128 devices in a mesh: grp: 4 (over x), dap: 32 (over y, z, core).
Axes of the slice: x: 4, y: 4, z: 4, core: 2. Of those that a mesh axis runs over, the one named last changes fastest.
Arguments:
- pair_state: bfloat16 [8, 512, 512, 128], P('grp', 'dap'), may hold values from -6 to 6
- lengths: int32 [8], replicated, may hold values from 128 to 512, as said below
- norm_gain: float32 [3, 128], replicated, may hold values from 0.1 to 1.9
- norm_shift: float32 [3, 128], replicated, may hold values from -3 to 3
- attn_proj: bfloat16 [2, 128, 512], replicated
- bias_proj: bfloat16 [2, 128, 4], replicated, may hold values from -1.5 to 1.5
- attn_out: bfloat16 [2, 128, 128], replicated, may hold values from -0.5 to 0.5
- trans_up: bfloat16 [128, 512], replicated, may hold values from -0.5 to 0.5
- trans_down: bfloat16 [512, 128], replicated, may hold values from -0.25 to 0.25
Outputs:
- pair_out: bfloat16 [8, 512, 512, 128], P('grp', 'dap')
The draws below stay inside these ranges and needn't reach their ends.
Inputs may be any that keep to these rules, and one draw needn't show every extreme that they name: `lengths`: residues of each protein; one protein has exactly 512.
All inputs are finite; a program needn't handle non-finite values.
Results may differ from the reference program's by a relative error of at most 0.035.
Values may be sent and summed in bfloat16 or wider, within the bound.
No kernel may reach another device: no remote copies, remote signals or barrier semaphores. Data moves between devices by JAX's collectives and lax.ppermute only.
A program may use at most 128 MiB of HBM per device.

```python
import jax
import jax.numpy as jnp
from jax import lax

PAIR = 128
HEADS = 4
HEAD_DIM = 32
TRANS = 512
PROTEINS = 8
RESIDUES = 512
ROW_BLOCK = 4


def draw_lengths(key, part):
    key = jax.random.fold_in(key, 11)
    first_key, second_key = jax.random.split(key)
    drawn = jax.random.randint(first_key, (PROTEINS,), RESIDUES // 4, RESIDUES + 1)
    longest = jax.random.randint(second_key, (), 0, PROTEINS)
    return jnp.where(jnp.arange(PROTEINS) == longest, RESIDUES, drawn).astype(jnp.int32)


def draw_attn_proj(key, part):
    key = jax.random.fold_in(key, 23)
    first_key = jax.random.fold_in(key, 0)
    values = jax.random.normal(first_key, (2, PAIR, 4 * PAIR), jnp.float32) * PAIR ** (-0.5)
    return values.astype(jnp.bfloat16)


def level_of(rng, extent, shards, smallest, top_value):
    gain = 1.0
    for position, blocks in shards:
        draws = jax.random.uniform(jax.random.fold_in(jax.random.fold_in(rng, 6), position), (blocks,), jnp.float32, smallest / len(shards), top_value / len(shards))
        gain = gain * jnp.repeat(jnp.exp(draws), extent[position] // blocks).reshape((-1,) + (1,) * (len(extent) - 1 - position))
    return gain


def bell_draw(key, shape, width, limit, cuts=(), kind=jnp.bfloat16):
    values = jax.random.normal(key, shape, jnp.float32) * width
    if len(cuts) > 0:
        values = level_of(key, shape, cuts, -0.22, 0.18) * values
    return jnp.clip(values, min=-limit, max=limit).astype(kind)


def setup_inputs(seed: int = 0) -> dict:
    streams_of = jax.random.split(jax.random.key(seed), 10)
    return {
        "pair_state": bell_draw(streams_of[0], (PROTEINS, RESIDUES, RESIDUES, PAIR), 1.0, 6.0, ((0, 4), (1, 32))),
        "lengths": draw_lengths(jax.random.fold_in(streams_of[9], 71), 0),
        "norm_gain": jnp.clip(1.0 + 0.18 * jax.random.normal(streams_of[2], (3, PAIR), jnp.float32), 0.1, 1.9),
        "norm_shift": bell_draw(streams_of[3], (3, PAIR), 0.5, 3.0, (), jnp.float32),
        "attn_proj": draw_attn_proj(jax.random.fold_in(streams_of[9], 71), 0),
        "bias_proj": bell_draw(streams_of[5], (2, PAIR, HEADS), (PAIR // 8) ** -0.5, 1.5),
        "attn_out": bell_draw(streams_of[6], (2, PAIR, PAIR), PAIR ** -0.5, 0.5),
        "trans_up": bell_draw(streams_of[7], (PAIR, TRANS), PAIR ** -0.5, 0.5),
        "trans_down": bell_draw(streams_of[8], (TRANS, PAIR), TRANS ** -0.5, 0.25),
    }


EPSILON = 1e-05
MASKED = -1000000000.0

def layer_norm(values, gain_row, shift_row):
    values = values.astype(jnp.float32)
    center = values - lax.optimization_barrier(jnp.mean(values, -1, keepdims=True))
    spread = lax.optimization_barrier(jnp.mean(center * center, -1, keepdims=True))
    return (center * lax.rsqrt(spread + EPSILON) * gain_row + shift_row).astype(jnp.bfloat16)

def block_update(normed, bias_full, length, start, proj_in, proj_out):
    width_all = normed.shape[1]
    chans = normed.shape[2]
    rows_in = lax.dynamic_slice_in_dim(normed, start, ROW_BLOCK, 0)
    projected = jnp.dot(rows_in.reshape(-1, chans), proj_in, preferred_element_type=jnp.float32)
    projected = projected.reshape(ROW_BLOCK, width_all, 4 * chans)
    query = (projected[..., :chans] * HEAD_DIM ** (-0.5)).astype(jnp.bfloat16).reshape(ROW_BLOCK, width_all, HEADS, HEAD_DIM)
    keyed = projected[..., chans:2 * chans].astype(jnp.bfloat16).reshape(ROW_BLOCK, width_all, HEADS, HEAD_DIM)
    valued = projected[..., 2 * chans:3 * chans].astype(jnp.bfloat16).reshape(ROW_BLOCK, width_all, HEADS, HEAD_DIM)
    gating = projected[..., 3 * chans:]
    scores = jnp.einsum('rjhd,rkhd->rhjk', query.astype(jnp.float32), keyed.astype(jnp.float32))
    scores = scores + bias_full.astype(jnp.float32)[None]
    live = jnp.arange(width_all, dtype=jnp.int32) < length
    scores = jnp.where(live, scores, MASKED)
    weights = jax.nn.softmax(scores, axis=-1).astype(jnp.bfloat16)
    mixed = jnp.einsum('rhjk,rkhd->rjhd', weights.astype(jnp.float32), valued.astype(jnp.float32))
    mixed = mixed.reshape(ROW_BLOCK, width_all, chans)
    gated = (mixed * jax.nn.sigmoid(gating)).astype(jnp.bfloat16)
    result = jnp.dot(gated.reshape(-1, chans), proj_out, preferred_element_type=jnp.float32)
    return result.reshape(ROW_BLOCK, width_all, chans)

def cell_mask(width_all, length):
    live = jnp.arange(width_all, dtype=jnp.int32) < length
    return (live[:, None] & live[None, :])[..., None]

def row_module(pair, length, gain_row, shift_row, proj_in, proj_bias, proj_out):
    width_all = pair.shape[0]
    normed = layer_norm(pair, gain_row, shift_row)
    bias_full = jnp.einsum('jkc,ch->hjk', normed.astype(jnp.float32), proj_bias.astype(jnp.float32)).astype(jnp.bfloat16)

    def one_block(start):
        return block_update(normed, bias_full, length, start, proj_in, proj_out)
    starts = jnp.arange(0, width_all, ROW_BLOCK, dtype=jnp.int32)
    update = lax.map(one_block, starts).reshape(pair.shape)
    update = jnp.where(cell_mask(width_all, length), update, 0.0)
    return (pair.astype(jnp.float32) + update).astype(jnp.bfloat16)

def transition(pair, length, gain_row, shift_row, up_proj, down_proj):
    width_all = pair.shape[0]
    chans = pair.shape[2]
    normed = layer_norm(pair, gain_row, shift_row)

    def one_block(start):
        rows_in = lax.dynamic_slice_in_dim(normed, start, ROW_BLOCK, 0)
        hidden_units = jax.nn.relu(jnp.dot(rows_in.reshape(-1, chans), up_proj, preferred_element_type=jnp.float32)).astype(jnp.bfloat16)
        result = jnp.dot(hidden_units, down_proj, preferred_element_type=jnp.float32)
        return result.reshape(ROW_BLOCK, width_all, chans)
    starts = jnp.arange(0, width_all, ROW_BLOCK, dtype=jnp.int32)
    update = lax.map(one_block, starts).reshape(pair.shape)
    update = jnp.where(cell_mask(width_all, length), update, 0.0)
    return (pair.astype(jnp.float32) + update).astype(jnp.bfloat16)

def reference(pair_state, lengths, norm_gain, norm_shift, attn_proj, bias_proj, attn_out, trans_up, trans_down):

    def protein(operands):
        pair, length = operands
        first = row_module(pair, length, norm_gain[0], norm_shift[0], attn_proj[0], bias_proj[0], attn_out[0])
        flipped = row_module(jnp.swapaxes(first, 0, 1), length, norm_gain[1], norm_shift[1], attn_proj[1], bias_proj[1], attn_out[1])
        second = jnp.swapaxes(flipped, 0, 1)
        return transition(second, length, norm_gain[2], norm_shift[2], trans_up, trans_down)
    return lax.map(protein, (pair_state, lengths))
```

```python
from functools import partial

import jax
import jax.numpy as jnp
from jax import lax
from jax.experimental import pallas as pl
from jax.experimental.pallas import tpu as pltpu
from jax.sharding import PartitionSpec as P

HEADS = 4
HEAD_DIM = 32
CHANS = 128
RES = 512
DEVS = 32
ROWS = 16
HIDDEN = 512
EPSILON = 1e-05
LOG2E = 1.4426950408889634
MASKED = -1e30
SAFE_SQUARED = 90.0**2
WIDTHS = (256, 384, 512)
BF = jnp.bfloat16
F32 = jnp.float32
VMEM_LIMIT = 48 * 2**20


def layer_norm(values, gain_row, shift_row):
    center = values - jnp.mean(values, -1, keepdims=True)
    spread = jnp.mean(center * center, -1, keepdims=True)
    return (center * lax.rsqrt(spread + EPSILON) * gain_row + shift_row).astype(BF)


def dot_nn(left, right):
    return jnp.dot(left, right, preferred_element_type=F32)


def dot_nt(left, right):
    return lax.dot_general(left, right, (((1,), (1,)), ((), ())), preferred_element_type=F32)


def first_bias_kernel(x_ref, gain_ref, shift_ref, bpt_ref, out_ref, rows_scr):
    r = pl.program_id(1)
    y = layer_norm(x_ref[0, 0].astype(F32), gain_ref[...], shift_ref[...])
    b = dot_nt(bpt_ref[...], y)
    for h in range(HEADS):
        rows_scr[pl.ds(h * ROWS + r, 1), :] = b[h : h + 1]

    @pl.when(r == ROWS - 1)
    def _():
        out_ref[0] = rows_scr[...].astype(BF)


def first_bias(state, gain, shift, bpt):
    pairs = state.shape[0]
    whole = lambda a: pl.BlockSpec(a.shape, lambda p, r: (0,) * a.ndim)
    return pl.pallas_call(
        first_bias_kernel,
        grid=(pairs, ROWS),
        in_specs=[pl.BlockSpec((1, 1, RES, CHANS), lambda p, r: (p, r, 0, 0))]
        + [whole(a) for a in (gain, shift, bpt)],
        out_specs=pl.BlockSpec((1, HEADS * ROWS, RES), lambda p, r: (p, 0, 0)),
        out_shape=jax.ShapeDtypeStruct((pairs, HEADS * ROWS, RES), BF),
        scratch_shapes=[pltpu.VMEM((HEADS * ROWS, RES), F32)],
        name="first_bias",
    )(state, gain, shift, bpt)


def attend_kernel(
    flipped,
    info_ref,
    x_ref,
    bias_ref,
    gain_ref,
    shift_ref,
    gain2_ref,
    shift2_ref,
    w_ref,
    wkt_ref,
    wo_ref,
    extra_ref,
    down_ref,
    out_ref,
    bias_out_ref,
    biasf,
    vblk,
    qm,
    kts,
    gate,
    mixed,
    line,
    bias_rows,
):
    step = pl.program_id(0)
    n = info_ref[0]
    row = info_ref[1] + step * info_ref[2]
    head_of = lax.broadcasted_iota(jnp.int32, (1, CHANS), 1) // HEAD_DIM

    def load_x(width):
        if flipped:
            return x_ref[: width // ROWS, 0].reshape(width, CHANS).astype(F32)
        return x_ref[0, :width].astype(F32)

    def load_rest(width):
        if flipped:
            return x_ref[width // ROWS :, 0].reshape(RES - width, CHANS).astype(F32)
        return x_ref[0, width:].astype(F32)

    @pl.when(step == 0)
    def _():
        klive = lax.broadcasted_iota(jnp.int32, (1, RES), 1) < n
        for h in range(HEADS):
            b = bias_ref[:, 0, h * ROWS : (h + 1) * ROWS].reshape(RES, RES).astype(F32)
            if flipped:
                b = b.T
            b = jnp.where(klive, b * LOG2E, MASKED)
            biasf[h] = b - jnp.max(b, -1, keepdims=True)
            vblk[h, :, CHANS:] = jnp.broadcast_to(
                (head_of == h).astype(F32).astype(BF), (RES, CHANS)
            )

    def put(start, values):
        size = values.shape[0]
        line[pl.ds(start * ROWS + step, size, stride=ROWS), :] = values

    def work(width):
        x = load_x(width)
        y = layer_norm(x, gain_ref[...], shift_ref[...])
        proj = dot_nn(y, w_ref[...])
        q = proj[:, :CHANS] * (HEAD_DIM**-0.5 * LOG2E)
        v = proj[:, CHANS : 2 * CHANS]
        gate[:width] = jax.nn.sigmoid(proj[:, 2 * CHANS :])
        kt = dot_nt(wkt_ref[...], y)
        kts[:, :width] = kt.astype(BF)
        for h in range(HEADS):
            qm[h, :width] = jnp.where(head_of == h, q, 0.0).astype(BF)
            vblk[h, :width, :CHANS] = jnp.where(head_of == h, v, 0.0).astype(BF)
        same = (
            lax.broadcasted_iota(jnp.int32, (CHANS, CHANS), 0) // HEAD_DIM == head_of
        ).astype(F32).astype(BF)
        q_top = jnp.max(dot_nn((q * q).astype(BF), same))
        k_top = jnp.max(jnp.sum((kt * kt).reshape(HEADS, HEAD_DIM, width), 1))
        acc = jnp.zeros((width, 2 * CHANS), F32)
        for h in range(HEADS):
            s = dot_nn(qm[h, :width], kts[:, :width]) + biasf[h, :width, :width]
            acc += dot_nn(jnp.exp2(s).astype(BF), vblk[h, :width])
        mixed[:width] = acc[:, :CHANS] / acc[:, CHANS:]

        @pl.when(jnp.logical_not(q_top * k_top < SAFE_SQUARED))
        def _():
            def block(t, _):
                at = pl.ds(pl.multiple_of(t * 128, 128), 128)
                acc = jnp.zeros((128, 2 * CHANS), F32)
                for h in range(HEADS):
                    s = dot_nn(qm[h, at], kts[:, :width]) + biasf[h, at, :width]
                    s = s - jnp.max(s, -1, keepdims=True)
                    acc += dot_nn(jnp.exp2(s).astype(BF), vblk[h, :width])
                mixed[at] = acc[:, :CHANS] / acc[:, CHANS:]
                return 0

            lax.fori_loop(0, width // 128, block, 0)

        gated = (mixed[:width] * gate[:width]).astype(BF)
        live = lax.broadcasted_iota(jnp.int32, (width, 1), 0) < n
        update = jnp.where(live, dot_nn(gated, wo_ref[...]), 0.0)
        result = (load_x(width) + update).astype(BF).astype(F32)
        normed = layer_norm(result, gain2_ref[...], shift2_ref[...])
        if flipped:
            hidden = jax.nn.relu(dot_nn(normed, extra_ref[...])).astype(BF)
            update = jnp.where(live, dot_nn(hidden, down_ref[...]), 0.0)
            put(0, result + update)
        else:
            put(0, result)
            b = dot_nt(extra_ref[...], normed)
            for h in range(HEADS):
                bias_rows[pl.ds(h * ROWS + step, 1), :width] = b[h : h + 1]
        if width < RES:
            put(width, load_rest(width))

    low = 0
    for width in WIDTHS:

        @pl.when((row < n) & (n > low) & (n <= width))
        def _(width=width):
            work(width)

        low = width

    @pl.when(row >= n)
    def _():
        put(0, load_x(RES))

    @pl.when(step == ROWS - 1)
    def _():
        if flipped:
            for d in range(DEVS):
                out_ref[d] = (
                    line[d * ROWS * ROWS : (d + 1) * ROWS * ROWS].reshape(ROWS, ROWS, CHANS).astype(BF)
                )
            bias_out_ref[...] = jnp.zeros_like(bias_out_ref)
        else:
            for c in range(ROWS):
                out_ref[:, c] = (
                    line[c * RES : (c + 1) * RES].reshape(DEVS, ROWS, CHANS).astype(BF)
                )
            bias_out_ref[...] = bias_rows[...].astype(BF)


def attend(flipped, member, info, state, bias, gain, shift, gain2, shift2, w, wkt, wo, extra, down):
    whole = lambda a: pl.BlockSpec(a.shape, lambda i, s: (0,) * a.ndim)
    if flipped:
        x_spec = pl.BlockSpec((DEVS, 1, ROWS, CHANS), lambda i, s: (0, i, 0, 0))
    else:
        x_spec = pl.BlockSpec((None, 1, RES, CHANS), lambda i, s: (member, i, 0, 0))
    bias_spec = pl.BlockSpec((DEVS, 1, HEADS * ROWS, RES), lambda i, s: (0, member, 0, 0))
    out_shape = jax.ShapeDtypeStruct((DEVS, ROWS, ROWS, CHANS), BF)
    bias_rows = 16 if flipped else HEADS * ROWS
    bias_shape = jax.ShapeDtypeStruct((bias_rows, RES), BF)
    return pl.pallas_call(
        partial(attend_kernel, flipped),
        grid_spec=pltpu.PrefetchScalarGridSpec(
            num_scalar_prefetch=1,
            grid=(ROWS,),
            in_specs=[x_spec, bias_spec]
            + [whole(a) for a in (gain, shift, gain2, shift2, w, wkt, wo, extra, down)],
            out_specs=[whole(out_shape), whole(bias_shape)],
            scratch_shapes=[
                pltpu.VMEM((HEADS, RES, RES), F32),
                pltpu.VMEM((HEADS, RES, 2 * CHANS), BF),
                pltpu.VMEM((HEADS, RES, CHANS), BF),
                pltpu.VMEM((CHANS, RES), BF),
                pltpu.VMEM((RES, CHANS), F32),
                pltpu.VMEM((RES, CHANS), F32),
                pltpu.VMEM((RES * ROWS, CHANS), F32),
                pltpu.VMEM((HEADS * ROWS, RES), F32),
            ],
        ),
        out_shape=[out_shape, bias_shape],
        compiler_params=pltpu.CompilerParams(vmem_limit_bytes=VMEM_LIMIT),
        cost_estimate=pl.CostEstimate(
            flops=30_000_000_000, bytes_accessed=8_000_000, transcendentals=0
        ),
        name="attend_columns" if flipped else "attend_rows",
    )(info, state, bias, gain, shift, gain2, shift2, w, wkt, wo, extra, down)


def join_kernel(x_ref, out_ref, line):
    for e in range(DEVS):
        line[pl.ds(e, ROWS, stride=DEVS), :] = x_ref[e, 0].astype(F32)
    out_ref[0] = line[...].astype(BF)


def join(state):
    return pl.pallas_call(
        join_kernel,
        grid=(ROWS,),
        in_specs=[pl.BlockSpec((DEVS, 1, ROWS, CHANS), lambda i: (0, i, 0, 0))],
        out_specs=pl.BlockSpec((1, RES, CHANS), lambda i: (i, 0, 0)),
        out_shape=jax.ShapeDtypeStruct((ROWS, RES, CHANS), BF),
        scratch_shapes=[pltpu.VMEM((RES, CHANS), F32)],
        name="join",
    )(state)


def swap_blocks(state):
    return lax.all_to_all(state, "dap", 0, 0, tiled=True)


def on_device(
    pair_state, lengths, norm_gain, norm_shift, attn_proj, bias_proj, attn_out, trans_up, trans_down
):
    group = lax.axis_index("grp")
    me = lax.axis_index("dap")
    pairs = pair_state.shape[0]
    gains = [norm_gain[m : m + 1] for m in range(3)]
    shifts = [norm_shift[m : m + 1] for m in range(3)]
    w_qvg = [
        jnp.concatenate([attn_proj[m, :, :CHANS], attn_proj[m, :, 2 * CHANS :]], 1)
        for m in range(2)
    ]
    w_kt = [attn_proj[m, :, CHANS : 2 * CHANS].T for m in range(2)]
    bpt = [jnp.pad(bias_proj[m].T, ((0, 16 - HEADS), (0, 0))) for m in range(2)]
    lens = [lax.dynamic_index_in_dim(lengths, group * pairs + p, 0, keepdims=False) for p in range(pairs)]
    row_info = [jnp.stack([n, me * ROWS, 1]).astype(jnp.int32) for n in lens]
    col_info = [jnp.stack([n, me, DEVS]).astype(jnp.int32) for n in lens]

    bias0 = lax.all_gather(first_bias(pair_state, gains[0], shifts[0], bpt[0]), "dap", axis=0)
    moved, bias1 = [], []
    for p in range(pairs):
        first, local = attend(
            False, p, row_info[p], pair_state, bias0, gains[0], shifts[0], gains[1], shifts[1],
            w_qvg[0], w_kt[0], attn_out[0], bpt[1], trans_down,
        )
        bias1.append(lax.all_gather(local[None], "dap", axis=0))
        moved.append(swap_blocks(first))
    outs = []
    for p in range(pairs):
        third, _ = attend(
            True, 0, col_info[p], moved[p], bias1[p], gains[1], shifts[1], gains[2], shifts[2],
            w_qvg[1], w_kt[1], attn_out[1], trans_up, trans_down,
        )
        outs.append(join(swap_blocks(third)))
    return jnp.stack(outs)


def solution(mesh):
    in_specs = (P("grp", "dap", None, None), P(), P(), P(), P(), P(), P(), P(), P())
    out_specs = P("grp", "dap", None, None)
    return jax.shard_map(
        on_device, mesh=mesh, in_specs=in_specs, out_specs=out_specs, check_vma=False
    )
```

```python
from functools import partial

import jax
import jax.numpy as jnp
from jax import lax
from jax.experimental import pallas as pl
from jax.experimental.pallas import tpu as pltpu
from jax.sharding import PartitionSpec as P

HEADS = 4
HEAD_DIM = 32
CHANS = 128
RES = 512
DEVS = 32
ROWS = 16
HIDDEN = 512
EPSILON = 1e-05
LOG2E = 1.4426950408889634
MASKED = -1e30
PARTS = 1
EXTRA = 8
COLUMN_CUTS = (((0, 16),), ((0, 16),))
DEN_LOW = 2.0**-60
DEN_HIGH = 2.0**60
WIDTHS = (256, 384, 512)
BF = jnp.bfloat16
F32 = jnp.float32
VMEM_LIMIT = 48 * 2**20


def dot_nn(left, right):
    return jnp.dot(left, right, preferred_element_type=F32)


def dot_nt(left, right):
    return lax.dot_general(left, right, (((1,), (1,)), ((), ())), preferred_element_type=F32)


def spread_norm(values, ones, gain_row, shift_row):
    wide = values.astype(F32)
    center = wide - jnp.mean(wide, -1, keepdims=True)
    spread = jnp.mean(center * center, -1, keepdims=True)
    return (center * lax.rsqrt(spread + EPSILON) * gain_row + shift_row).astype(BF)


def mean_matrix():
    return jnp.full((CHANS, CHANS), 1.0 / CHANS, F32).astype(BF)


def first_bias_kernel(x_ref, gain_ref, shift_ref, bpt_ref, out_ref, rows_scr):
    ones = mean_matrix()

    def one_row(r, _):
        y = spread_norm(x_ref[r], ones, gain_ref[...], shift_ref[...])
        b = dot_nt(bpt_ref[...], y)
        for h in range(HEADS):
            rows_scr[pl.ds(h * ROWS + r, 1), :] = b[h : h + 1]
        return 0

    lax.fori_loop(0, ROWS, one_row, 0, unroll=2)
    out_ref[...] = rows_scr[...].astype(BF)


def first_bias(member, state, gain, shift, bpt):
    whole = lambda a: pl.BlockSpec(a.shape, lambda i: (0,) * a.ndim)
    return pl.pallas_call(
        first_bias_kernel,
        grid=(1,),
        in_specs=[pl.BlockSpec((None, ROWS, RES, CHANS), lambda i: (member, 0, 0, 0))]
        + [whole(a) for a in (gain, shift, bpt)],
        out_specs=pl.BlockSpec((HEADS * ROWS, RES), lambda i: (0, 0)),
        out_shape=jax.ShapeDtypeStruct((HEADS * ROWS, RES), BF),
        scratch_shapes=[pltpu.VMEM((HEADS * ROWS, RES), F32)],
        compiler_params=pltpu.CompilerParams(vmem_limit_bytes=VMEM_LIMIT),
        name="first_bias",
    )(state, gain, shift, bpt)


def attend_kernel(
    flipped,
    column,
    count,
    info_ref,
    x_ref,
    bias_ref,
    bias_more_ref,
    gain_ref,
    shift_ref,
    gain2_ref,
    shift2_ref,
    w_ref,
    wkt_ref,
    wo_ref,
    extra_ref,
    down_ref,
    out_ref,
    biasf,
    vblk_a,
    vblk_b,
    qm_a,
    qm_b,
    kts_a,
    kts_b,
    gate_a,
    gate_b,
    gated_a,
    gated_b,
    line,
    bias_rows,
    low_den,
    high_den,
):
    n = info_ref[0]
    first_row = info_ref[1]
    stride = info_ref[2]
    parity = info_ref[3]
    live_rows = jnp.clip((n - first_row + stride - 1) // stride - column, 0, count)
    head_of = lax.broadcasted_iota(jnp.int32, (1, CHANS), 1) // HEAD_DIM
    ones = mean_matrix()
    side_a = (vblk_a, qm_a, kts_a, gate_a)
    side_b = (vblk_b, qm_b, kts_b, gate_b)

    def load_x(r, start, size):
        if flipped:
            return x_ref[start // ROWS : (start + size) // ROWS, column + r].reshape(size, CHANS)
        return x_ref[r, start : start + size]

    def put(r, start, values):
        line[pl.ds(start * count + r, values.shape[0], stride=count), :] = values

    klive = lax.broadcasted_iota(jnp.int32, (1, RES), 1) < n
    def hold(h, at, b):
        b = jnp.where(klive, b.astype(F32) * LOG2E, MASKED)
        biasf[h, at] = b - jnp.max(b, -1, keepdims=True)

    if flipped:
        for ref, base, first_head in (
            (bias_ref, 0, 2 * parity),
            (bias_more_ref, 0, 2 - 2 * parity),
        ):
            for t in range(EXTRA):
                q = t % 4
                b = ref[:, base + t].reshape(RES, CHANS).astype(F32).T
                hold(first_head + t // 4, slice(q * CHANS, (q + 1) * CHANS), b)
    else:

        def place(t, _):
            for ref, base in ((bias_ref, 4), (bias_more_ref, 4 + DEVS // 2)):
                at = pl.ds(pl.multiple_of(info_ref[base + t] * ROWS, ROWS), ROWS)
                for h in range(HEADS):
                    hold(h, at, ref[t, h * ROWS : (h + 1) * ROWS])
            return 0

        lax.fori_loop(0, DEVS // 2, place, 0, unroll=2)
    for h in range(HEADS):
        tail = jnp.broadcast_to((head_of == h).astype(F32).astype(BF), (RES, CHANS))
        vblk_a[h, :, CHANS:] = tail
        vblk_b[h, :, CHANS:] = tail
    low_den[...] = jnp.ones_like(low_den)
    high_den[...] = jnp.ones_like(high_den)

    def prologue(r, side, start, size):
        vblk, qm, kts, gate = side
        at = slice(start, start + size)
        y = spread_norm(load_x(r, start, size), ones, gain_ref[...], shift_ref[...])
        proj = dot_nn(y, w_ref[...])
        q = proj[:, :CHANS] * (HEAD_DIM**-0.5 * LOG2E)
        v = proj[:, CHANS : 2 * CHANS]
        gate[at] = jax.nn.sigmoid(proj[:, 2 * CHANS :])
        kts[:, at] = dot_nt(wkt_ref[...], y).astype(BF)
        for h in range(HEADS):
            qm[h, at] = jnp.where(head_of == h, q, 0.0).astype(BF)
            vblk[h, at, :CHANS] = jnp.where(head_of == h, v, 0.0).astype(BF)

    def one_head(side, h, width):
        vblk, qm, kts, _ = side
        s = dot_nn(qm[h, :width], kts[:, :width]) + biasf[h, :width, :width]
        return dot_nn(jnp.exp2(s).astype(BF), vblk[h, :width])

    def finish_heads(acc, side, gated, width):
        den = acc[:, CHANS:]
        live = lax.broadcasted_iota(jnp.int32, (width, 1), 0) < n
        shown = jnp.where(live, den, 1.0).reshape(width // 8, 8, CHANS)
        low_den[...] = jnp.minimum(low_den[...], jnp.min(shown, 0))
        high_den[...] = jnp.maximum(high_den[...], jnp.max(shown, 0))
        gated[:width] = (acc[:, :CHANS] / den * side[3][:width]).astype(BF)

    def epilogue(r, gated, start, size):
        live = start + lax.broadcasted_iota(jnp.int32, (size, 1), 0) < n
        update = jnp.where(live, dot_nn(gated[start : start + size], wo_ref[...]), 0.0)
        result = (load_x(r, start, size).astype(F32) + update).astype(BF)
        normed = spread_norm(result, ones, gain2_ref[...], shift2_ref[...])
        wide = result.astype(F32)
        if flipped:
            hidden = jax.nn.relu(dot_nn(normed, extra_ref[...])).astype(BF)
            update = jnp.where(live, dot_nn(hidden, down_ref[...]), 0.0)
            put(r, start, wide + update)
        else:
            put(r, start, wide)
            b = dot_nt(extra_ref[...], normed)
            for h in range(HEADS):
                bias_rows[pl.ds(h * ROWS + r, 1), start : start + size] = b[h : h + 1]

    def work(width):
        part = width // PARTS
        chunks = [c * part for c in range(PARTS)]

        def row(r, side, gated):
            for c in chunks:
                prologue(r, side, c, part)
            acc = one_head(side, 0, width)
            for h in range(1, HEADS):
                acc = acc + one_head(side, h, width)
            finish_heads(acc, side, gated, width)
            for c in chunks:
                epilogue(r, gated, c, part)

        def pro(r, side):
            for c in chunks:
                prologue(r, side, c, part)

        def att(side, gated, hook=None):
            acc = one_head(side, 0, width)
            for h in range(1, HEADS):
                if hook is not None:
                    hook(h)
                acc = acc + one_head(side, h, width)
            finish_heads(acc, side, gated, width)

        def epi(r, gated):
            for c in chunks:
                epilogue(r, gated, c, part)

        def pair(u, _):
            ra, rb = 2 * u, 2 * u + 1
            pro(ra, side_a)
            pro(rb, side_b)
            att(side_a, gated_a)
            att(side_b, gated_b)
            epi(ra, gated_a)
            epi(rb, gated_b)
            return 0

        lax.fori_loop(0, live_rows // 2, pair, 0)

        @pl.when(live_rows % 2 == 1)
        def _():
            row(live_rows - 1, side_a, gated_a)

        if width < RES:

            def rest(r, _):
                put(r, width, load_x(r, width, RES - width).astype(F32))
                return 0

            lax.fori_loop(0, live_rows, rest, 0)

        @pl.when(jnp.logical_not((jnp.min(low_den[...]) > DEN_LOW) & (jnp.max(high_den[...]) < DEN_HIGH)))
        def _():
            def careful(r, _):
                for c in chunks:
                    prologue(r, side_a, c, part)

                def block(t, _):
                    at = pl.ds(pl.multiple_of(t * 128, 128), 128)
                    acc = jnp.zeros((128, 2 * CHANS), F32)
                    for h in range(HEADS):
                        s = dot_nn(qm_a[h, at], kts_a[:, :width]) + biasf[h, at, :width]
                        s = s - jnp.max(s, -1, keepdims=True)
                        acc += dot_nn(jnp.exp2(s).astype(BF), vblk_a[h, :width])
                    gated_a[at] = (acc[:, :CHANS] / acc[:, CHANS:] * gate_a[at]).astype(BF)
                    return 0

                lax.fori_loop(0, width // 128, block, 0)
                for c in chunks:
                    epilogue(r, gated_a, c, part)
                return 0

            lax.fori_loop(0, live_rows, careful, 0)

    low = 0
    for width in WIDTHS:

        @pl.when((live_rows > 0) & (n > low) & (n <= width))
        def _(width=width):
            work(width)

        low = width

    def passed(r, _):
        put(r, 0, load_x(r, 0, RES).astype(F32))
        return 0

    lax.fori_loop(live_rows, count, passed, 0)

    def deliver(c, _):
        if flipped:
            size = ROWS * count * 2
            at = pl.ds(pl.multiple_of(c * size, size), size)
            out_ref[pl.ds(2 * c, 2)] = line[at].reshape(2, ROWS, count, CHANS).astype(BF)
        else:
            at = pl.ds(pl.multiple_of(c * RES, RES), RES)
            out_ref[:, c] = line[at].reshape(DEVS, ROWS, CHANS).astype(BF)
        return 0

    lax.fori_loop(0, ROWS, deliver, 0)
    if not flipped:
        for h in range(HEADS):
            for q in range(4):
                piece = bias_rows[h * ROWS : (h + 1) * ROWS, q * CHANS : (q + 1) * CHANS].astype(BF)
                for e in range(h // 2, DEVS, 2):
                    out_ref[e, ROWS + (h % 2) * 4 + q] = piece


def attend(flipped, place, info, state, biases, gain, shift, gain2, shift2, w, wkt, wo, extra, down):
    whole = lambda a: pl.BlockSpec(a.shape, lambda i, s: (0,) * a.ndim)
    if flipped:
        column, count = place
        x_spec = pl.BlockSpec((DEVS, ROWS, ROWS, CHANS), lambda i, s: (0, 0, 0, 0))
        bias_specs = [
            pl.BlockSpec((DEVS, EXTRA, ROWS, CHANS), lambda i, s, at=at: (0, at, 0, 0))
            for _, at in biases
        ]
        out_shape = jax.ShapeDtypeStruct((DEVS, ROWS, count, CHANS), BF)
    else:
        column, count = 0, ROWS
        x_spec = pl.BlockSpec((None, ROWS, RES, CHANS), lambda i, s: (place, 0, 0, 0))
        bias_specs = [
            pl.BlockSpec((DEVS // 2, HEADS * ROWS, RES), lambda i, s, at=at: (at, 0, 0))
            for _, at in biases
        ]
        out_shape = jax.ShapeDtypeStruct((DEVS, ROWS + EXTRA, ROWS, CHANS), BF)
    twice = lambda shape, dtype: [pltpu.VMEM(shape, dtype)] * 2
    return pl.pallas_call(
        partial(attend_kernel, flipped, column, count),
        grid_spec=pltpu.PrefetchScalarGridSpec(
            num_scalar_prefetch=1,
            grid=(1,),
            in_specs=[x_spec]
            + bias_specs
            + [whole(a) for a in (gain, shift, gain2, shift2, w, wkt, wo, extra, down)],
            out_specs=whole(out_shape),
            scratch_shapes=[pltpu.VMEM((HEADS, RES, RES), F32)]
            + twice((HEADS, RES, 2 * CHANS), BF)
            + twice((HEADS, RES, CHANS), BF)
            + twice((CHANS, RES), BF)
            + twice((RES, CHANS), F32)
            + twice((RES, CHANS), BF)
            + [
                pltpu.VMEM((RES * count, CHANS), F32),
                pltpu.VMEM((HEADS * ROWS, RES), F32),
            ]
            + twice((8, CHANS), F32),
        ),
        out_shape=out_shape,
        compiler_params=pltpu.CompilerParams(vmem_limit_bytes=VMEM_LIMIT),
        cost_estimate=pl.CostEstimate(
            flops=30_000_000_000, bytes_accessed=8_000_000, transcendentals=0
        ),
        name="attend_columns" if flipped else "attend_rows",
    )(info, state, biases[0][0], biases[1][0], gain, shift, gain2, shift2, w, wkt, wo, extra, down)


def tail_kernel(x_ref, *refs):
    refs[-1][...] = x_ref[...]


def bias_tail(state, after):
    shape = (DEVS, EXTRA, ROWS, CHANS)
    return pl.pallas_call(
        tail_kernel,
        grid=(1,),
        in_specs=[pl.BlockSpec(shape, lambda i: (0, ROWS // EXTRA, 0, 0))]
        + [pl.BlockSpec(memory_space=pl.ANY)] * len(after),
        out_specs=pl.BlockSpec(shape, lambda i: (0, 0, 0, 0)),
        out_shape=jax.ShapeDtypeStruct(shape, BF),
        name="bias_tail",
    )(state, *after)


def join_kernel(parts, *refs):
    out_ref, line = refs[-2:]

    def one_row(i, _):
        start = 0
        for ref in refs[:parts]:
            size = ref.shape[2]
            for e in range(DEVS):
                line[pl.ds(start * DEVS + e, size, stride=DEVS), :] = ref[e, i].astype(F32)
            start += size
        out_ref[i] = line[...].astype(BF)
        return 0

    lax.fori_loop(0, ROWS, one_row, 0)


def join(member, pieces, earlier):
    more = [] if earlier is None else [earlier]
    return pl.pallas_call(
        partial(join_kernel, len(pieces)),
        grid=(1,),
        in_specs=[pl.BlockSpec(a.shape, lambda i: (0, 0, 0, 0)) for a in pieces]
        + [pl.BlockSpec(memory_space=pl.ANY)] * len(more),
        out_specs=pl.BlockSpec((None, ROWS, RES, CHANS), lambda i: (member, 0, 0, 0)),
        out_shape=jax.ShapeDtypeStruct((2, ROWS, RES, CHANS), BF),
        scratch_shapes=[pltpu.VMEM((RES, CHANS), F32)],
        input_output_aliases={len(pieces): 0} if more else {},
        compiler_params=pltpu.CompilerParams(vmem_limit_bytes=VMEM_LIMIT),
        name="join",
    )(*pieces, *more)


def shifted(state, dy, dz, dc):
    return lax.ppermute(
        state,
        "dap",
        [
            ((y * 4 + z) * 2 + c, ((y + dy) % 4 * 4 + (z + dz) % 4) * 2 + (c ^ dc))
            for y in range(4)
            for z in range(4)
            for c in range(2)
        ],
    )


SHIFTS = (0, 1, -1, 2)


def stack_kernel(*refs):
    out_ref = refs[-1]
    for t in range(len(SHIFTS)):
        out_ref[t] = refs[t][...]


def stack_blocks(blocks, after):
    return pl.pallas_call(
        stack_kernel,
        in_specs=[pl.BlockSpec(memory_space=pltpu.VMEM)] * len(blocks)
        + [pl.BlockSpec(memory_space=pl.ANY)],
        out_specs=pl.BlockSpec(memory_space=pltpu.VMEM),
        out_shape=jax.ShapeDtypeStruct((len(blocks),) + blocks[0].shape, BF),
        name="stack_blocks",
    )(*blocks, after)


def gather_steps(local, after):
    line = stack_blocks([local] + [shifted(local, 0, k, 0) for k in SHIFTS[1:]], after)
    plane = jnp.concatenate([line] + [shifted(line, k, 0, 0) for k in SHIFTS[1:]])
    return plane, shifted(plane, 0, 0, 1)


def gather_order(me):
    y, z, c = me // 8, me // 2 % 4, me % 2
    order = [
        ((y - ky) % 4 * 4 + (z - kz) % 4) * 2 + (c ^ other if other else c)
        for other in range(2)
        for ky in SHIFTS
        for kz in SHIFTS
    ]
    return [jnp.asarray(v, jnp.int32) for v in order]


def swap_blocks(state):
    return lax.all_to_all(state, "dap", 0, 0, tiled=True)


def on_device(
    pair_state, lengths, norm_gain, norm_shift, attn_proj, bias_proj, attn_out, trans_up, trans_down
):
    group = lax.axis_index("grp")
    me = lax.axis_index("dap")
    pairs = pair_state.shape[0]
    gains = [norm_gain[m : m + 1] for m in range(3)]
    shifts = [norm_shift[m : m + 1] for m in range(3)]
    w_qvg = [
        jnp.concatenate([attn_proj[m, :, :CHANS], attn_proj[m, :, 2 * CHANS :]], 1)
        for m in range(2)
    ]
    w_kt = [attn_proj[m, :, CHANS : 2 * CHANS].T for m in range(2)]
    bpt = [jnp.pad(bias_proj[m].T, ((0, 16 - HEADS), (0, 0))) for m in range(2)]
    lens = [lax.dynamic_index_in_dim(lengths, group * pairs + p, 0, keepdims=False) for p in range(pairs)]
    parity = me % 2
    order = [gather_order(me)] + [list(range(DEVS))] * (pairs - 1)
    row_info = [
        jnp.stack([jnp.asarray(v, jnp.int32) for v in [n, me * ROWS, 1, parity] + o])
        for n, o in zip(lens, order)
    ]
    col_info = [jnp.stack([jnp.asarray(v, jnp.int32) for v in [n, me, DEVS, parity]]) for n in lens]

    bias0 = [first_bias(p, pair_state, gains[0], shifts[0], bpt[0]) for p in range(pairs)]
    first_plane, second_plane = gather_steps(bias0[0], bias0[1])
    whole_bias = lax.all_gather(bias0[1], "dap", axis=0)
    biases = [[(first_plane, 0), (second_plane, 0)], [(whole_bias, 0), (whole_bias, 1)]]
    moved = []
    for p in range(pairs):
        first = attend(
            False, p, row_info[p], pair_state, biases[p], gains[0], shifts[0], gains[1], shifts[1],
            w_qvg[0], w_kt[0], attn_out[0], bpt[1], trans_down,
        )
        moved.append(swap_blocks(first))
    result, pieces, third = None, [], None
    for p in range(pairs):
        other = shifted(bias_tail(moved[p], pieces and [third]), 0, 0, 1)
        pieces = []
        for place in COLUMN_CUTS[p]:
            third = attend(
                True, place, col_info[p], moved[p], [(moved[p], 2), (other, 0)], gains[1], shifts[1],
                gains[2], shifts[2], w_qvg[1], w_kt[1], attn_out[1], trans_up, trans_down,
            )
            pieces.append(swap_blocks(third))
        result = join(p, pieces, result)
    return result


def solution(mesh):
    in_specs = (P("grp", "dap", None, None), P(), P(), P(), P(), P(), P(), P(), P())
    out_specs = P("grp", "dap", None, None)
    return jax.shard_map(
        on_device, mesh=mesh, in_specs=in_specs, out_specs=out_specs, check_vma=False
    )
```

```python
from functools import partial

import jax
import jax.numpy as jnp
from jax import lax
from jax.experimental import pallas as pl
from jax.experimental.pallas import tpu as pltpu
from jax.sharding import PartitionSpec as P

HEADS = 4
HEAD_DIM = 32
CHANS = 128
RES = 512
DEVS = 32
ROWS = 16
HIDDEN = 512
EPSILON = 1e-05
LOG2E = 1.4426950408889634
MASKED = -1e30
PARTS = 1
EXTRA = 8
COLUMN_CUTS = (((0, 16),), ((0, 16),))
DEN_LOW = 2.0**-60
DEN_HIGH = 2.0**60
WIDTHS = (256, 384, 512)
BF = jnp.bfloat16
F32 = jnp.float32
VMEM_LIMIT = 48 * 2**20


def dot_nn(left, right):
    return jnp.dot(left, right, preferred_element_type=F32)


def dot_nt(left, right):
    return lax.dot_general(left, right, (((1,), (1,)), ((), ())), preferred_element_type=F32)


def spread_norm(values, ones, gain_row, shift_row):
    wide = values.astype(F32)
    center = wide - jnp.mean(wide, -1, keepdims=True)
    spread = jnp.mean(center * center, -1, keepdims=True)
    return (center * lax.rsqrt(spread + EPSILON) * gain_row + shift_row).astype(BF)


def mean_matrix():
    return jnp.full((CHANS, CHANS), 1.0 / CHANS, F32).astype(BF)


def first_bias_kernel(x_ref, gain_ref, shift_ref, bpt_ref, out_ref, rows_scr):
    ones = mean_matrix()

    def one_row(r, _):
        y = spread_norm(x_ref[r], ones, gain_ref[...], shift_ref[...])
        b = dot_nt(bpt_ref[...], y)
        for h in range(HEADS):
            rows_scr[pl.ds(h * ROWS + r, 1), :] = b[h : h + 1]
        return 0

    lax.fori_loop(0, ROWS, one_row, 0, unroll=2)
    out_ref[...] = rows_scr[...].astype(BF)


def first_bias(member, state, gain, shift, bpt):
    whole = lambda a: pl.BlockSpec(a.shape, lambda i: (0,) * a.ndim)
    return pl.pallas_call(
        first_bias_kernel,
        grid=(1,),
        in_specs=[pl.BlockSpec((None, ROWS, RES, CHANS), lambda i: (member, 0, 0, 0))]
        + [whole(a) for a in (gain, shift, bpt)],
        out_specs=pl.BlockSpec((HEADS * ROWS, RES), lambda i: (0, 0)),
        out_shape=jax.ShapeDtypeStruct((HEADS * ROWS, RES), BF),
        scratch_shapes=[pltpu.VMEM((HEADS * ROWS, RES), F32)],
        compiler_params=pltpu.CompilerParams(vmem_limit_bytes=VMEM_LIMIT),
        name="first_bias",
    )(state, gain, shift, bpt)


def attend_kernel(
    flipped,
    column,
    count,
    info_ref,
    x_ref,
    bias_ref,
    bias_more_ref,
    gain_ref,
    shift_ref,
    gain2_ref,
    shift2_ref,
    w_ref,
    wkt_ref,
    wo_ref,
    extra_ref,
    down_ref,
    out_ref,
    biasf,
    vblk_a,
    vblk_b,
    qm_a,
    qm_b,
    kts_a,
    kts_b,
    gate_a,
    gate_b,
    gated_a,
    gated_b,
    line,
    bias_rows,
    low_den,
    high_den,
):
    n = info_ref[0]
    first_row = info_ref[1]
    stride = info_ref[2]
    parity = info_ref[3]
    live_rows = jnp.clip((n - first_row + stride - 1) // stride - column, 0, count)
    head_of = lax.broadcasted_iota(jnp.int32, (1, CHANS), 1) // HEAD_DIM
    ones = mean_matrix()
    side_a = (vblk_a, qm_a, kts_a, gate_a)
    side_b = (vblk_b, qm_b, kts_b, gate_b)

    def load_x(r, start, size):
        if flipped:
            return x_ref[start // ROWS : (start + size) // ROWS, column + r].reshape(size, CHANS)
        return x_ref[r, start : start + size]

    def put(r, start, values):
        line[pl.ds(start * count + r, values.shape[0], stride=count), :] = values

    klive = lax.broadcasted_iota(jnp.int32, (1, RES), 1) < n
    def hold(h, at, b):
        b = jnp.where(klive, b.astype(F32) * LOG2E, MASKED)
        biasf[h, at] = b - jnp.max(b, -1, keepdims=True)

    if flipped:
        for ref, base, first_head in (
            (bias_ref, 0, 2 * parity),
            (bias_more_ref, 0, 2 - 2 * parity),
        ):
            for t in range(EXTRA):
                q = t % 4
                b = ref[:, base + t].reshape(RES, CHANS).astype(F32).T
                hold(first_head + t // 4, slice(q * CHANS, (q + 1) * CHANS), b)
    else:

        def place(t, _):
            for ref, base in ((bias_ref, 4), (bias_more_ref, 4 + DEVS // 2)):
                at = pl.ds(pl.multiple_of(info_ref[base + t] * ROWS, ROWS), ROWS)
                for h in range(HEADS):
                    hold(h, at, ref[t, h * ROWS : (h + 1) * ROWS])
            return 0

        lax.fori_loop(0, DEVS // 2, place, 0, unroll=2)
    for h in range(HEADS):
        tail = jnp.broadcast_to((head_of == h).astype(F32).astype(BF), (RES, CHANS))
        vblk_a[h, :, CHANS:] = tail
        vblk_b[h, :, CHANS:] = tail
    low_den[...] = jnp.ones_like(low_den)
    high_den[...] = jnp.ones_like(high_den)

    def prologue(r, side, start, size):
        vblk, qm, kts, gate = side
        at = slice(start, start + size)
        y = spread_norm(load_x(r, start, size), ones, gain_ref[...], shift_ref[...])
        proj = dot_nn(y, w_ref[...])
        q = proj[:, :CHANS] * (HEAD_DIM**-0.5 * LOG2E)
        v = proj[:, CHANS : 2 * CHANS]
        gate[at] = jax.nn.sigmoid(proj[:, 2 * CHANS :])
        kts[:, at] = dot_nt(wkt_ref[...], y).astype(BF)
        for h in range(HEADS):
            qm[h, at] = jnp.where(head_of == h, q, 0.0).astype(BF)
            vblk[h, at, :CHANS] = jnp.where(head_of == h, v, 0.0).astype(BF)

    def one_head(side, h, width):
        vblk, qm, kts, _ = side
        s = dot_nn(qm[h, :width], kts[:, :width]) + biasf[h, :width, :width]
        return dot_nn(jnp.exp2(s).astype(BF), vblk[h, :width])

    def finish_heads(acc, side, gated, width):
        den = acc[:, CHANS:]
        live = lax.broadcasted_iota(jnp.int32, (width, 1), 0) < n
        shown = jnp.where(live, den, 1.0).reshape(width // 8, 8, CHANS)
        low_den[...] = jnp.minimum(low_den[...], jnp.min(shown, 0))
        high_den[...] = jnp.maximum(high_den[...], jnp.max(shown, 0))
        gated[:width] = (acc[:, :CHANS] / den * side[3][:width]).astype(BF)

    def epilogue(r, gated, start, size):
        live = start + lax.broadcasted_iota(jnp.int32, (size, 1), 0) < n
        update = jnp.where(live, dot_nn(gated[start : start + size], wo_ref[...]), 0.0)
        result = (load_x(r, start, size).astype(F32) + update).astype(BF)
        normed = spread_norm(result, ones, gain2_ref[...], shift2_ref[...])
        wide = result.astype(F32)
        if flipped:
            hidden = jax.nn.relu(dot_nn(normed, extra_ref[...])).astype(BF)
            update = jnp.where(live, dot_nn(hidden, down_ref[...]), 0.0)
            put(r, start, wide + update)
        else:
            put(r, start, wide)
            b = dot_nt(extra_ref[...], normed)
            for h in range(HEADS):
                bias_rows[pl.ds(h * ROWS + r, 1), start : start + size] = b[h : h + 1]

    def work(width):
        part = width // PARTS
        chunks = [c * part for c in range(PARTS)]

        def row(r, side, gated):
            for c in chunks:
                prologue(r, side, c, part)
            acc = one_head(side, 0, width)
            for h in range(1, HEADS):
                acc = acc + one_head(side, h, width)
            finish_heads(acc, side, gated, width)
            for c in chunks:
                epilogue(r, gated, c, part)

        def pro(r, side):
            for c in chunks:
                prologue(r, side, c, part)

        def att(side, gated, hook=None):
            acc = one_head(side, 0, width)
            for h in range(1, HEADS):
                if hook is not None:
                    hook(h)
                acc = acc + one_head(side, h, width)
            finish_heads(acc, side, gated, width)

        def epi(r, gated):
            for c in chunks:
                epilogue(r, gated, c, part)

        def pair(u, _):
            ra, rb = 2 * u, 2 * u + 1
            pro(ra, side_a)
            pro(rb, side_b)
            att(side_a, gated_a)
            att(side_b, gated_b)
            epi(ra, gated_a)
            epi(rb, gated_b)
            return 0

        lax.fori_loop(0, live_rows // 2, pair, 0)

        @pl.when(live_rows % 2 == 1)
        def _():
            row(live_rows - 1, side_a, gated_a)

        if width < RES:

            def rest(r, _):
                put(r, width, load_x(r, width, RES - width).astype(F32))
                return 0

            lax.fori_loop(0, live_rows, rest, 0)

        @pl.when(jnp.logical_not((jnp.min(low_den[...]) > DEN_LOW) & (jnp.max(high_den[...]) < DEN_HIGH)))
        def _():
            def careful(r, _):
                for c in chunks:
                    prologue(r, side_a, c, part)

                def block(t, _):
                    at = pl.ds(pl.multiple_of(t * 128, 128), 128)
                    acc = jnp.zeros((128, 2 * CHANS), F32)
                    for h in range(HEADS):
                        s = dot_nn(qm_a[h, at], kts_a[:, :width]) + biasf[h, at, :width]
                        s = s - jnp.max(s, -1, keepdims=True)
                        acc += dot_nn(jnp.exp2(s).astype(BF), vblk_a[h, :width])
                    gated_a[at] = (acc[:, :CHANS] / acc[:, CHANS:] * gate_a[at]).astype(BF)
                    return 0

                lax.fori_loop(0, width // 128, block, 0)
                for c in chunks:
                    epilogue(r, gated_a, c, part)
                return 0

            lax.fori_loop(0, live_rows, careful, 0)

    low = 0
    for width in WIDTHS:

        @pl.when((live_rows > 0) & (n > low) & (n <= width))
        def _(width=width):
            work(width)

        low = width

    def passed(r, _):
        put(r, 0, load_x(r, 0, RES).astype(F32))
        return 0

    lax.fori_loop(live_rows, count, passed, 0)

    def deliver(c, _):
        if flipped:
            size = ROWS * count * 2
            at = pl.ds(pl.multiple_of(c * size, size), size)
            out_ref[pl.ds(2 * c, 2)] = line[at].reshape(2, ROWS, count, CHANS).astype(BF)
        else:
            at = pl.ds(pl.multiple_of(c * RES, RES), RES)
            out_ref[:, c] = line[at].reshape(DEVS, ROWS, CHANS).astype(BF)
        return 0

    lax.fori_loop(0, ROWS, deliver, 0)
    if not flipped:
        for h in range(HEADS):
            for q in range(4):
                piece = bias_rows[h * ROWS : (h + 1) * ROWS, q * CHANS : (q + 1) * CHANS].astype(BF)
                for e in range(h // 2, DEVS, 2):
                    out_ref[e, ROWS + (h % 2) * 4 + q] = piece


def attend(flipped, place, info, state, biases, gain, shift, gain2, shift2, w, wkt, wo, extra, down):
    whole = lambda a: pl.BlockSpec(a.shape, lambda i, s: (0,) * a.ndim)
    if flipped:
        column, count = place
        x_spec = pl.BlockSpec((DEVS, ROWS, ROWS, CHANS), lambda i, s: (0, 0, 0, 0))
        bias_specs = [
            pl.BlockSpec((DEVS, EXTRA, ROWS, CHANS), lambda i, s, at=at: (0, at, 0, 0))
            for _, at in biases
        ]
        out_shape = jax.ShapeDtypeStruct((DEVS, ROWS, count, CHANS), BF)
    else:
        column, count = 0, ROWS
        x_spec = pl.BlockSpec((None, ROWS, RES, CHANS), lambda i, s: (place, 0, 0, 0))
        bias_specs = [
            pl.BlockSpec((DEVS // 2, HEADS * ROWS, RES), lambda i, s, at=at: (at, 0, 0))
            for _, at in biases
        ]
        out_shape = jax.ShapeDtypeStruct((DEVS, ROWS + EXTRA, ROWS, CHANS), BF)
    twice = lambda shape, dtype: [pltpu.VMEM(shape, dtype)] * 2
    return pl.pallas_call(
        partial(attend_kernel, flipped, column, count),
        grid_spec=pltpu.PrefetchScalarGridSpec(
            num_scalar_prefetch=1,
            grid=(1,),
            in_specs=[x_spec]
            + bias_specs
            + [whole(a) for a in (gain, shift, gain2, shift2, w, wkt, wo, extra, down)],
            out_specs=whole(out_shape),
            scratch_shapes=[pltpu.VMEM((HEADS, RES, RES), F32)]
            + twice((HEADS, RES, 2 * CHANS), BF)
            + twice((HEADS, RES, CHANS), BF)
            + twice((CHANS, RES), BF)
            + twice((RES, CHANS), F32)
            + twice((RES, CHANS), BF)
            + [
                pltpu.VMEM((RES * count, CHANS), F32),
                pltpu.VMEM((HEADS * ROWS, RES), F32),
            ]
            + twice((8, CHANS), F32),
        ),
        out_shape=out_shape,
        compiler_params=pltpu.CompilerParams(vmem_limit_bytes=VMEM_LIMIT),
        cost_estimate=pl.CostEstimate(
            flops=30_000_000_000, bytes_accessed=8_000_000, transcendentals=0
        ),
        name="attend_columns" if flipped else "attend_rows",
    )(info, state, biases[0][0], biases[1][0], gain, shift, gain2, shift2, w, wkt, wo, extra, down)


def tail_kernel(x_ref, *refs):
    refs[-1][...] = x_ref[...]


def bias_tail(state, after):
    shape = (DEVS, EXTRA, ROWS, CHANS)
    return pl.pallas_call(
        tail_kernel,
        grid=(1,),
        in_specs=[pl.BlockSpec(shape, lambda i: (0, ROWS // EXTRA, 0, 0))]
        + [pl.BlockSpec(memory_space=pl.ANY)] * len(after),
        out_specs=pl.BlockSpec(shape, lambda i: (0, 0, 0, 0)),
        out_shape=jax.ShapeDtypeStruct(shape, BF),
        name="bias_tail",
    )(state, *after)


def join_kernel(parts, *refs):
    out_ref, line = refs[-2:]

    def one_row(i, _):
        start = 0
        for ref in refs[:parts]:
            size = ref.shape[2]
            for e in range(DEVS):
                line[pl.ds(start * DEVS + e, size, stride=DEVS), :] = ref[e, i].astype(F32)
            start += size
        out_ref[i] = line[...].astype(BF)
        return 0

    lax.fori_loop(0, ROWS, one_row, 0)


def join(member, pieces, earlier):
    more = [] if earlier is None else [earlier]
    return pl.pallas_call(
        partial(join_kernel, len(pieces)),
        grid=(1,),
        in_specs=[pl.BlockSpec(a.shape, lambda i: (0, 0, 0, 0)) for a in pieces]
        + [pl.BlockSpec(memory_space=pl.ANY)] * len(more),
        out_specs=pl.BlockSpec((None, ROWS, RES, CHANS), lambda i: (member, 0, 0, 0)),
        out_shape=jax.ShapeDtypeStruct((2, ROWS, RES, CHANS), BF),
        scratch_shapes=[pltpu.VMEM((RES, CHANS), F32)],
        input_output_aliases={len(pieces): 0} if more else {},
        compiler_params=pltpu.CompilerParams(vmem_limit_bytes=VMEM_LIMIT),
        name="join",
    )(*pieces, *more)


def shifted(state, dy, dz, dc):
    return lax.ppermute(
        state,
        "dap",
        [
            ((y * 4 + z) * 2 + c, ((y + dy) % 4 * 4 + (z + dz) % 4) * 2 + (c ^ dc))
            for y in range(4)
            for z in range(4)
            for c in range(2)
        ],
    )


SHIFTS = (0, 1, -1, 2)


def stack_kernel(*refs):
    out_ref = refs[-1]
    for t in range(len(SHIFTS)):
        out_ref[t] = refs[t][...]


def stack_blocks(blocks, after):
    return pl.pallas_call(
        stack_kernel,
        in_specs=[pl.BlockSpec(memory_space=pltpu.VMEM)] * len(blocks)
        + [pl.BlockSpec(memory_space=pl.ANY)],
        out_specs=pl.BlockSpec(memory_space=pltpu.VMEM),
        out_shape=jax.ShapeDtypeStruct((len(blocks),) + blocks[0].shape, BF),
        name="stack_blocks",
    )(*blocks, after)


def gather_steps(local, after):
    line = stack_blocks([local] + [shifted(local, 0, k, 0) for k in SHIFTS[1:]], after)
    plane = jnp.concatenate([line] + [shifted(line, k, 0, 0) for k in SHIFTS[1:]])
    return plane, shifted(plane, 0, 0, 1)


def gather_order(me):
    y, z, c = me // 8, me // 2 % 4, me % 2
    order = [
        ((y - ky) % 4 * 4 + (z - kz) % 4) * 2 + (c ^ other if other else c)
        for other in range(2)
        for ky in SHIFTS
        for kz in SHIFTS
    ]
    return [jnp.asarray(v, jnp.int32) for v in order]


def swap_blocks(state):
    return lax.all_to_all(state, "dap", 0, 0, tiled=True)


def on_device(
    pair_state, lengths, norm_gain, norm_shift, attn_proj, bias_proj, attn_out, trans_up, trans_down
):
    group = lax.axis_index("grp")
    me = lax.axis_index("dap")
    pairs = pair_state.shape[0]
    gains = [norm_gain[m : m + 1] for m in range(3)]
    shifts = [norm_shift[m : m + 1] for m in range(3)]
    w_qvg = [
        jnp.concatenate([attn_proj[m, :, :CHANS], attn_proj[m, :, 2 * CHANS :]], 1)
        for m in range(2)
    ]
    w_kt = [attn_proj[m, :, CHANS : 2 * CHANS].T for m in range(2)]
    bpt = [jnp.pad(bias_proj[m].T, ((0, 16 - HEADS), (0, 0))) for m in range(2)]
    lens = [lax.dynamic_index_in_dim(lengths, group * pairs + p, 0, keepdims=False) for p in range(pairs)]
    parity = me % 2
    order = [gather_order(me)] + [list(range(DEVS))] * (pairs - 1)
    row_info = [
        jnp.stack([jnp.asarray(v, jnp.int32) for v in [n, me * ROWS, 1, parity] + o])
        for n, o in zip(lens, order)
    ]
    col_info = [jnp.stack([jnp.asarray(v, jnp.int32) for v in [n, me, DEVS, parity]]) for n in lens]

    bias0 = [first_bias(p, pair_state, gains[0], shifts[0], bpt[0]) for p in range(pairs)]
    first_plane, second_plane = gather_steps(bias0[0], bias0[1])
    whole_bias = lax.all_gather(bias0[1], "dap", axis=0)
    biases = [[(first_plane, 0), (second_plane, 0)], [(whole_bias, 0), (whole_bias, 1)]]
    firsts, moved = [], []
    for p in range(pairs):
        first = attend(
            False, p, row_info[p], pair_state, biases[p], gains[0], shifts[0], gains[1], shifts[1],
            w_qvg[0], w_kt[0], attn_out[0], bpt[1], trans_down,
        )
        firsts.append(first)
        moved.append(swap_blocks(first))
    result, third = None, firsts[-1]
    for p in range(pairs):
        other = shifted(bias_tail(moved[p], [third]), 0, 0, 1)
        pieces = []
        for place in COLUMN_CUTS[p]:
            third = attend(
                True, place, col_info[p], moved[p], [(moved[p], 2), (other, 0)], gains[1], shifts[1],
                gains[2], shifts[2], w_qvg[1], w_kt[1], attn_out[1], trans_up, trans_down,
            )
            pieces.append(swap_blocks(third))
        result = join(p, pieces, result)
    return result


def solution(mesh):
    in_specs = (P("grp", "dap", None, None), P(), P(), P(), P(), P(), P(), P(), P())
    out_specs = P("grp", "dap", None, None)
    return jax.shard_map(
        on_device, mesh=mesh, in_specs=in_specs, out_specs=out_specs, check_vma=False
    )
```

```python
from functools import partial

import jax
import jax.numpy as jnp
from jax import lax
from jax.experimental import pallas as pl
from jax.experimental.pallas import tpu as pltpu
from jax.sharding import PartitionSpec as P

HEADS = 4
HEAD_DIM = 32
CHANS = 128
RES = 512
DEVS = 32
ROWS = 16
HIDDEN = 512
EPSILON = 1e-05
LOG2E = 1.4426950408889634
MASKED = -1e30
PARTS = 1
EXTRA = 8
DEN_LOW = 2.0**-60
DEN_HIGH = 2.0**60
WIDTHS = (256, 384, 512)
BF = jnp.bfloat16
F32 = jnp.float32
VMEM_LIMIT = 48 * 2**20


def dot_nn(left, right):
    return jnp.dot(left, right, preferred_element_type=F32)


def dot_nt(left, right):
    return lax.dot_general(left, right, (((1,), (1,)), ((), ())), preferred_element_type=F32)


def spread_norm(values, ones, gain_row, shift_row):
    wide = values.astype(F32)
    center = wide - jnp.mean(wide, -1, keepdims=True)
    spread = jnp.mean(center * center, -1, keepdims=True)
    return (center * lax.rsqrt(spread + EPSILON) * gain_row + shift_row).astype(BF)


def mean_matrix():
    return jnp.full((CHANS, CHANS), 1.0 / CHANS, F32).astype(BF)


def first_bias_kernel(_, x_ref, gain_ref, shift_ref, bpt_ref, out_ref, rows_scr):
    ones = mean_matrix()

    def one_row(r, _):
        y = spread_norm(x_ref[r], ones, gain_ref[...], shift_ref[...])
        b = dot_nt(bpt_ref[...], y)
        for h in range(HEADS):
            rows_scr[pl.ds(h * ROWS + r, 1), :] = b[h : h + 1]
        return 0

    lax.fori_loop(0, ROWS, one_row, 0, unroll=2)
    out_ref[...] = rows_scr[...].astype(BF)


def first_bias(info, state, gain, shift, bpt):
    whole = lambda a: pl.BlockSpec(a.shape, lambda i, s: (0,) * a.ndim)
    return pl.pallas_call(
        first_bias_kernel,
        grid_spec=pltpu.PrefetchScalarGridSpec(
            num_scalar_prefetch=1,
            grid=(1,),
            in_specs=[pl.BlockSpec((None, ROWS, RES, CHANS), lambda i, s: (s[4], 0, 0, 0))]
            + [whole(a) for a in (gain, shift, bpt)],
            out_specs=pl.BlockSpec((HEADS * ROWS, RES), lambda i, s: (0, 0)),
            scratch_shapes=[pltpu.VMEM((HEADS * ROWS, RES), F32)],
        ),
        out_shape=jax.ShapeDtypeStruct((HEADS * ROWS, RES), BF),
        compiler_params=pltpu.CompilerParams(vmem_limit_bytes=VMEM_LIMIT),
        name="first_bias",
    )(info, state, gain, shift, bpt)


def attend_kernel(
    flipped,
    column,
    count,
    info_ref,
    x_ref,
    bias_ref,
    bias_more_ref,
    gain_ref,
    shift_ref,
    gain2_ref,
    shift2_ref,
    w_ref,
    wkt_ref,
    wo_ref,
    extra_ref,
    down_ref,
    out_ref,
    biasf,
    vblk_a,
    vblk_b,
    qm_a,
    qm_b,
    kts_a,
    kts_b,
    gate_a,
    gate_b,
    gated_a,
    gated_b,
    line,
    bias_rows,
    low_den,
    high_den,
):
    n = info_ref[0]
    first_row = info_ref[1]
    stride = info_ref[2]
    parity = info_ref[3]
    live_rows = jnp.clip((n - first_row + stride - 1) // stride - column, 0, count)
    head_of = lax.broadcasted_iota(jnp.int32, (1, CHANS), 1) // HEAD_DIM
    ones = mean_matrix()
    side_a = (vblk_a, qm_a, kts_a, gate_a)
    side_b = (vblk_b, qm_b, kts_b, gate_b)

    def load_x(r, start, size):
        if flipped:
            return x_ref[start // ROWS : (start + size) // ROWS, column + r].reshape(size, CHANS)
        return x_ref[r, start : start + size]

    def put(r, start, values):
        line[pl.ds(start * count + r, values.shape[0], stride=count), :] = values

    klive = lax.broadcasted_iota(jnp.int32, (1, RES), 1) < n
    def hold(h, at, b):
        b = jnp.where(klive, b.astype(F32) * LOG2E, MASKED)
        biasf[h, at] = b - jnp.max(b, -1, keepdims=True)

    if flipped:
        for ref, base, first_head in (
            (bias_ref, 0, 2 * parity),
            (bias_more_ref, 0, 2 - 2 * parity),
        ):
            for t in range(EXTRA):
                q = t % 4
                b = ref[:, base + t].reshape(RES, CHANS).astype(F32).T
                hold(first_head + t // 4, slice(q * CHANS, (q + 1) * CHANS), b)
    else:

        def place(t, _):
            for ref, base in ((bias_ref, 5), (bias_more_ref, 5 + DEVS // 2)):
                at = pl.ds(pl.multiple_of(info_ref[base + t] * ROWS, ROWS), ROWS)
                for h in range(HEADS):
                    hold(h, at, ref[t, h * ROWS : (h + 1) * ROWS])
            return 0

        lax.fori_loop(0, DEVS // 2, place, 0, unroll=2)
    for h in range(HEADS):
        tail = jnp.broadcast_to((head_of == h).astype(F32).astype(BF), (RES, CHANS))
        vblk_a[h, :, CHANS:] = tail
        vblk_b[h, :, CHANS:] = tail
    low_den[...] = jnp.ones_like(low_den)
    high_den[...] = jnp.ones_like(high_den)

    def prologue(r, side, start, size):
        vblk, qm, kts, gate = side
        at = slice(start, start + size)
        y = spread_norm(load_x(r, start, size), ones, gain_ref[...], shift_ref[...])
        proj = dot_nn(y, w_ref[...])
        q = proj[:, :CHANS] * (HEAD_DIM**-0.5 * LOG2E)
        v = proj[:, CHANS : 2 * CHANS]
        gate[at] = jax.nn.sigmoid(proj[:, 2 * CHANS :])
        kts[:, at] = dot_nt(wkt_ref[...], y).astype(BF)
        for h in range(HEADS):
            qm[h, at] = jnp.where(head_of == h, q, 0.0).astype(BF)
            vblk[h, at, :CHANS] = jnp.where(head_of == h, v, 0.0).astype(BF)

    def one_head(side, h, width):
        vblk, qm, kts, _ = side
        s = dot_nn(qm[h, :width], kts[:, :width]) + biasf[h, :width, :width]
        return dot_nn(jnp.exp2(s).astype(BF), vblk[h, :width])

    def finish_heads(acc, side, gated, width):
        den = acc[:, CHANS:]
        live = lax.broadcasted_iota(jnp.int32, (width, 1), 0) < n
        shown = jnp.where(live, den, 1.0).reshape(width // 8, 8, CHANS)
        low_den[...] = jnp.minimum(low_den[...], jnp.min(shown, 0))
        high_den[...] = jnp.maximum(high_den[...], jnp.max(shown, 0))
        gated[:width] = (acc[:, :CHANS] / den * side[3][:width]).astype(BF)

    def epilogue(r, gated, start, size):
        live = start + lax.broadcasted_iota(jnp.int32, (size, 1), 0) < n
        update = jnp.where(live, dot_nn(gated[start : start + size], wo_ref[...]), 0.0)
        result = (load_x(r, start, size).astype(F32) + update).astype(BF)
        normed = spread_norm(result, ones, gain2_ref[...], shift2_ref[...])
        wide = result.astype(F32)
        if flipped:
            hidden = jax.nn.relu(dot_nn(normed, extra_ref[...])).astype(BF)
            update = jnp.where(live, dot_nn(hidden, down_ref[...]), 0.0)
            put(r, start, wide + update)
        else:
            put(r, start, wide)
            b = dot_nt(extra_ref[...], normed)
            for h in range(HEADS):
                bias_rows[pl.ds(h * ROWS + r, 1), start : start + size] = b[h : h + 1]

    def work(width):
        part = width // PARTS
        chunks = [c * part for c in range(PARTS)]

        def row(r, side, gated):
            for c in chunks:
                prologue(r, side, c, part)
            acc = one_head(side, 0, width)
            for h in range(1, HEADS):
                acc = acc + one_head(side, h, width)
            finish_heads(acc, side, gated, width)
            for c in chunks:
                epilogue(r, gated, c, part)

        def pro(r, side):
            for c in chunks:
                prologue(r, side, c, part)

        def att(side, gated, hook=None):
            acc = one_head(side, 0, width)
            for h in range(1, HEADS):
                if hook is not None:
                    hook(h)
                acc = acc + one_head(side, h, width)
            finish_heads(acc, side, gated, width)

        def epi(r, gated):
            for c in chunks:
                epilogue(r, gated, c, part)

        def pair(u, _):
            ra, rb = 2 * u, 2 * u + 1
            pro(ra, side_a)
            pro(rb, side_b)
            att(side_a, gated_a)
            att(side_b, gated_b)
            epi(ra, gated_a)
            epi(rb, gated_b)
            return 0

        lax.fori_loop(0, live_rows // 2, pair, 0)

        @pl.when(live_rows % 2 == 1)
        def _():
            row(live_rows - 1, side_a, gated_a)

        if width < RES:

            def rest(r, _):
                put(r, width, load_x(r, width, RES - width).astype(F32))
                return 0

            lax.fori_loop(0, live_rows, rest, 0)

        @pl.when(jnp.logical_not((jnp.min(low_den[...]) > DEN_LOW) & (jnp.max(high_den[...]) < DEN_HIGH)))
        def _():
            def careful(r, _):
                for c in chunks:
                    prologue(r, side_a, c, part)

                def block(t, _):
                    at = pl.ds(pl.multiple_of(t * 128, 128), 128)
                    acc = jnp.zeros((128, 2 * CHANS), F32)
                    for h in range(HEADS):
                        s = dot_nn(qm_a[h, at], kts_a[:, :width]) + biasf[h, at, :width]
                        s = s - jnp.max(s, -1, keepdims=True)
                        acc += dot_nn(jnp.exp2(s).astype(BF), vblk_a[h, :width])
                    gated_a[at] = (acc[:, :CHANS] / acc[:, CHANS:] * gate_a[at]).astype(BF)
                    return 0

                lax.fori_loop(0, width // 128, block, 0)
                for c in chunks:
                    epilogue(r, gated_a, c, part)
                return 0

            lax.fori_loop(0, live_rows, careful, 0)

    low = 0
    for width in WIDTHS:

        @pl.when((live_rows > 0) & (n > low) & (n <= width))
        def _(width=width):
            work(width)

        low = width

    def passed(r, _):
        put(r, 0, load_x(r, 0, RES).astype(F32))
        return 0

    lax.fori_loop(live_rows, count, passed, 0)

    def deliver(c, _):
        if flipped:
            size = ROWS * count * 2
            at = pl.ds(pl.multiple_of(c * size, size), size)
            out_ref[pl.ds(2 * c, 2)] = line[at].reshape(2, ROWS, count, CHANS).astype(BF)
        else:
            at = pl.ds(pl.multiple_of(c * RES, RES), RES)
            out_ref[:, c] = line[at].reshape(DEVS, ROWS, CHANS).astype(BF)
        return 0

    lax.fori_loop(0, ROWS, deliver, 0)
    if not flipped:
        for h in range(HEADS):
            for q in range(4):
                piece = bias_rows[h * ROWS : (h + 1) * ROWS, q * CHANS : (q + 1) * CHANS].astype(BF)
                for e in range(h // 2, DEVS, 2):
                    out_ref[e, ROWS + (h % 2) * 4 + q] = piece


def attend(flipped, place, info, state, biases, gain, shift, gain2, shift2, w, wkt, wo, extra, down):
    whole = lambda a: pl.BlockSpec(a.shape, lambda i, s: (0,) * a.ndim)
    if flipped:
        column, count = place
        x_spec = pl.BlockSpec((DEVS, ROWS, ROWS, CHANS), lambda i, s: (0, 0, 0, 0))
        bias_specs = [
            pl.BlockSpec((DEVS, EXTRA, ROWS, CHANS), lambda i, s, at=at: (0, at, 0, 0))
            for _, at in biases
        ]
        out_shape = jax.ShapeDtypeStruct((DEVS, ROWS, count, CHANS), BF)
    else:
        column, count = 0, ROWS
        x_spec = pl.BlockSpec((None, ROWS, RES, CHANS), lambda i, s: (s[4], 0, 0, 0))
        bias_specs = [
            pl.BlockSpec((DEVS // 2, HEADS * ROWS, RES), lambda i, s, at=at: (at, 0, 0))
            for _, at in biases
        ]
        out_shape = jax.ShapeDtypeStruct((DEVS, ROWS + EXTRA, ROWS, CHANS), BF)
    twice = lambda shape, dtype: [pltpu.VMEM(shape, dtype)] * 2
    return pl.pallas_call(
        partial(attend_kernel, flipped, column, count),
        grid_spec=pltpu.PrefetchScalarGridSpec(
            num_scalar_prefetch=1,
            grid=(1,),
            in_specs=[x_spec]
            + bias_specs
            + [whole(a) for a in (gain, shift, gain2, shift2, w, wkt, wo, extra, down)],
            out_specs=whole(out_shape),
            scratch_shapes=[pltpu.VMEM((HEADS, RES, RES), F32)]
            + twice((HEADS, RES, 2 * CHANS), BF)
            + twice((HEADS, RES, CHANS), BF)
            + twice((CHANS, RES), BF)
            + twice((RES, CHANS), F32)
            + twice((RES, CHANS), BF)
            + [
                pltpu.VMEM((RES * count, CHANS), F32),
                pltpu.VMEM((HEADS * ROWS, RES), F32),
            ]
            + twice((8, CHANS), F32),
        ),
        out_shape=out_shape,
        compiler_params=pltpu.CompilerParams(vmem_limit_bytes=VMEM_LIMIT),
        cost_estimate=pl.CostEstimate(
            flops=30_000_000_000, bytes_accessed=8_000_000, transcendentals=0
        ),
        name="attend_columns" if flipped else "attend_rows",
    )(info, state, biases[0][0], biases[1][0], gain, shift, gain2, shift2, w, wkt, wo, extra, down)


def tail_kernel(x_ref, *refs):
    refs[-1][...] = x_ref[...]


def bias_tail(state, after):
    shape = (DEVS, EXTRA, ROWS, CHANS)
    return pl.pallas_call(
        tail_kernel,
        grid=(1,),
        in_specs=[pl.BlockSpec(shape, lambda i: (0, ROWS // EXTRA, 0, 0))]
        + [pl.BlockSpec(memory_space=pl.ANY)] * len(after),
        out_specs=pl.BlockSpec(shape, lambda i: (0, 0, 0, 0)),
        out_shape=jax.ShapeDtypeStruct(shape, BF),
        name="bias_tail",
    )(state, *after)


def join_kernel(_, x_ref, *refs):
    out_ref, line = refs[-2:]

    def one_row(i, _):
        for e in range(DEVS):
            line[pl.ds(e, ROWS, stride=DEVS), :] = x_ref[e, i].astype(F32)
        out_ref[i] = line[...].astype(BF)
        return 0

    lax.fori_loop(0, out_ref.shape[0], one_row, 0)


def join(info, state, earlier):
    more = [] if earlier is None else [earlier]
    part = ROWS // 4
    return pl.pallas_call(
        join_kernel,
        grid_spec=pltpu.PrefetchScalarGridSpec(
            num_scalar_prefetch=1,
            grid=(ROWS // part,),
            in_specs=[pl.BlockSpec((DEVS, part, ROWS, CHANS), lambda i, s: (0, i, 0, 0))]
            + [pl.BlockSpec(memory_space=pl.ANY)] * len(more),
            out_specs=pl.BlockSpec((None, part, RES, CHANS), lambda i, s: (s[4], i, 0, 0)),
            scratch_shapes=[pltpu.VMEM((RES, CHANS), F32)],
        ),
        out_shape=jax.ShapeDtypeStruct((2, ROWS, RES, CHANS), BF),
        input_output_aliases={2: 0} if more else {},
        compiler_params=pltpu.CompilerParams(vmem_limit_bytes=VMEM_LIMIT),
        name="join",
    )(info, state, *more)


def shifted(state, dy, dz, dc):
    return lax.ppermute(
        state,
        "dap",
        [
            ((y * 4 + z) * 2 + c, ((y + dy) % 4 * 4 + (z + dz) % 4) * 2 + (c ^ dc))
            for y in range(4)
            for z in range(4)
            for c in range(2)
        ],
    )


SHIFTS = (0, 1, -1, 2)


def stack_kernel(*refs):
    out_ref = refs[-1]
    for t in range(len(SHIFTS)):
        out_ref[t] = refs[t][...]


def stack_blocks(blocks, after):
    return pl.pallas_call(
        stack_kernel,
        in_specs=[pl.BlockSpec(memory_space=pltpu.VMEM)] * len(blocks)
        + [pl.BlockSpec(memory_space=pl.ANY)],
        out_specs=pl.BlockSpec(memory_space=pltpu.VMEM),
        out_shape=jax.ShapeDtypeStruct((len(blocks),) + blocks[0].shape, BF),
        name="stack_blocks",
    )(*blocks, after)


def gather_steps(local, after):
    line = stack_blocks([local] + [shifted(local, 0, k, 0) for k in SHIFTS[1:]], after)
    plane = jnp.concatenate([line] + [shifted(line, k, 0, 0) for k in SHIFTS[1:]])
    return plane, shifted(plane, 0, 0, 1)


def gather_order(me):
    y, z, c = me // 8, me // 2 % 4, me % 2
    order = [
        ((y - ky) % 4 * 4 + (z - kz) % 4) * 2 + (c ^ other if other else c)
        for other in range(2)
        for ky in SHIFTS
        for kz in SHIFTS
    ]
    return [jnp.asarray(v, jnp.int32) for v in order]


def swap_blocks(state):
    return lax.all_to_all(state, "dap", 0, 0, tiled=True)


def on_device(
    pair_state, lengths, norm_gain, norm_shift, attn_proj, bias_proj, attn_out, trans_up, trans_down
):
    group = lax.axis_index("grp")
    me = lax.axis_index("dap")
    pairs = pair_state.shape[0]
    gains = [norm_gain[m : m + 1] for m in range(3)]
    shifts = [norm_shift[m : m + 1] for m in range(3)]
    w_qvg = [
        jnp.concatenate([attn_proj[m, :, :CHANS], attn_proj[m, :, 2 * CHANS :]], 1)
        for m in range(2)
    ]
    w_kt = [attn_proj[m, :, CHANS : 2 * CHANS].T for m in range(2)]
    bpt = [jnp.pad(bias_proj[m].T, ((0, 16 - HEADS), (0, 0))) for m in range(2)]
    own = [lax.dynamic_index_in_dim(lengths, group * pairs + p, 0, keepdims=False) for p in range(pairs)]
    turned = (own[1] > own[0]).astype(jnp.int32)
    lens = [jnp.maximum(own[0], own[1]), jnp.minimum(own[0], own[1])]
    members = [turned, 1 - turned]
    parity = me % 2
    order = [gather_order(me)] + [list(range(DEVS))] * (pairs - 1)
    row_info = [
        jnp.stack([jnp.asarray(v, jnp.int32) for v in [n, me * ROWS, 1, parity, at] + o])
        for n, at, o in zip(lens, members, order)
    ]
    col_info = [
        jnp.stack([jnp.asarray(v, jnp.int32) for v in [n, me, DEVS, parity, at]])
        for n, at in zip(lens, members)
    ]

    bias0 = [first_bias(row_info[p], pair_state, gains[0], shifts[0], bpt[0]) for p in range(pairs)]
    first_plane, second_plane = gather_steps(bias0[0], bias0[1])
    whole_bias = lax.all_gather(bias0[1], "dap", axis=0)
    biases = [[(first_plane, 0), (second_plane, 0)], [(whole_bias, 0), (whole_bias, 1)]]
    firsts, moved = [], []
    for p in range(pairs):
        first = attend(
            False, None, row_info[p], pair_state, biases[p], gains[0], shifts[0], gains[1], shifts[1],
            w_qvg[0], w_kt[0], attn_out[0], bpt[1], trans_down,
        )
        firsts.append(first)
        moved.append(swap_blocks(first))
    result, third = None, firsts[-1]
    for p in range(pairs):
        other = shifted(bias_tail(moved[p], [third]), 0, 0, 1)
        third = attend(
            True, (0, ROWS), col_info[p], moved[p], [(moved[p], 2), (other, 0)], gains[1], shifts[1],
            gains[2], shifts[2], w_qvg[1], w_kt[1], attn_out[1], trans_up, trans_down,
        )
        result = join(col_info[p], swap_blocks(third), result)
    return result


def solution(mesh):
    in_specs = (P("grp", "dap", None, None), P(), P(), P(), P(), P(), P(), P(), P())
    out_specs = P("grp", "dap", None, None)
    return jax.shard_map(
        on_device, mesh=mesh, in_specs=in_specs, out_specs=out_specs, check_vma=False
    )
```

```python
from functools import partial

import jax
import jax.numpy as jnp
from jax import lax
from jax.experimental import pallas as pl
from jax.experimental.pallas import tpu as pltpu
from jax.sharding import PartitionSpec as P

HEADS = 4
HEAD_DIM = 32
CHANS = 128
RES = 512
DEVS = 32
ROWS = 16
HIDDEN = 512
EPSILON = 1e-05
LOG2E = 1.4426950408889634
MASKED = -1e30
PARTS = 1
EXTRA = 8
DEN_LOW = 2.0**-60
DEN_HIGH = 2.0**60
WIDTHS = (256, 384, 512)
BF = jnp.bfloat16
F32 = jnp.float32
VMEM_LIMIT = 48 * 2**20


def dot_nn(left, right):
    return jnp.dot(left, right, preferred_element_type=F32)


def dot_nt(left, right):
    return lax.dot_general(left, right, (((1,), (1,)), ((), ())), preferred_element_type=F32)


def spread_norm(values, ones, gain_row, shift_row):
    wide = values.astype(F32)
    center = wide - jnp.mean(wide, -1, keepdims=True)
    spread = jnp.mean(center * center, -1, keepdims=True)
    return (center * lax.rsqrt(spread + EPSILON) * gain_row + shift_row).astype(BF)


def mean_matrix():
    return jnp.full((CHANS, CHANS), 1.0 / CHANS, F32).astype(BF)


def first_bias_kernel(_, x_ref, gain_ref, shift_ref, bpt_ref, out_ref, rows_scr):
    ones = mean_matrix()

    def one_row(r, _):
        y = spread_norm(x_ref[r], ones, gain_ref[...], shift_ref[...])
        b = dot_nt(bpt_ref[...], y)
        for h in range(HEADS):
            rows_scr[pl.ds(h * ROWS + r, 1), :] = b[h : h + 1]
        return 0

    lax.fori_loop(0, ROWS, one_row, 0, unroll=2)
    out_ref[...] = rows_scr[...].astype(BF)


def first_bias(info, state, gain, shift, bpt):
    whole = lambda a: pl.BlockSpec(a.shape, lambda i, s: (0,) * a.ndim)
    return pl.pallas_call(
        first_bias_kernel,
        grid_spec=pltpu.PrefetchScalarGridSpec(
            num_scalar_prefetch=1,
            grid=(1,),
            in_specs=[pl.BlockSpec((None, ROWS, RES, CHANS), lambda i, s: (s[0], 0, 0, 0))]
            + [whole(a) for a in (gain, shift, bpt)],
            out_specs=pl.BlockSpec((HEADS * ROWS, RES), lambda i, s: (0, 0)),
            scratch_shapes=[pltpu.VMEM((HEADS * ROWS, RES), F32)],
        ),
        out_shape=jax.ShapeDtypeStruct((HEADS * ROWS, RES), BF),
        compiler_params=pltpu.CompilerParams(vmem_limit_bytes=VMEM_LIMIT),
        name="first_bias",
    )(info, state, gain, shift, bpt)


def attend_kernel(
    flipped,
    column,
    count,
    info_ref,
    x_ref,
    bias_ref,
    bias_more_ref,
    gain_ref,
    shift_ref,
    gain2_ref,
    shift2_ref,
    w_ref,
    wkt_ref,
    wo_ref,
    extra_ref,
    down_ref,
    out_ref,
    biasf,
    vblk_a,
    vblk_b,
    qm_a,
    qm_b,
    kts_a,
    kts_b,
    gate_a,
    gate_b,
    gated_a,
    gated_b,
    line,
    bias_rows,
    low_den,
    high_den,
):
    n = info_ref[0]
    first_row = info_ref[1]
    stride = info_ref[2]
    parity = info_ref[3]
    live_rows = jnp.clip((n - first_row + stride - 1) // stride - column, 0, count)
    head_of = lax.broadcasted_iota(jnp.int32, (1, CHANS), 1) // HEAD_DIM
    ones = mean_matrix()
    side_a = (vblk_a, qm_a, kts_a, gate_a)
    side_b = (vblk_b, qm_b, kts_b, gate_b)

    def load_x(r, start, size):
        if flipped:
            return x_ref[start // ROWS : (start + size) // ROWS, column + r].reshape(size, CHANS)
        return x_ref[r, start : start + size]

    def put(r, start, values):
        line[pl.ds(start * count + r, values.shape[0], stride=count), :] = values

    klive = lax.broadcasted_iota(jnp.int32, (1, RES), 1) < n
    def hold(h, at, b):
        b = jnp.where(klive, b.astype(F32) * LOG2E, MASKED)
        biasf[h, at] = b - jnp.max(b, -1, keepdims=True)

    if flipped:
        for ref, base, first_head in (
            (bias_ref, 0, 2 * parity),
            (bias_more_ref, 0, 2 - 2 * parity),
        ):
            for t in range(EXTRA):
                q = t % 4
                b = ref[:, base + t].reshape(RES, CHANS).astype(F32).T
                hold(first_head + t // 4, slice(q * CHANS, (q + 1) * CHANS), b)
    else:

        def place(t, _):
            for ref, base in ((bias_ref, 5), (bias_more_ref, 5 + DEVS // 2)):
                at = pl.ds(pl.multiple_of(info_ref[base + t] * ROWS, ROWS), ROWS)
                for h in range(HEADS):
                    hold(h, at, ref[t, h * ROWS : (h + 1) * ROWS])
            return 0

        lax.fori_loop(0, DEVS // 2, place, 0, unroll=2)
    for h in range(HEADS):
        tail = jnp.broadcast_to((head_of == h).astype(F32).astype(BF), (RES, CHANS))
        vblk_a[h, :, CHANS:] = tail
        vblk_b[h, :, CHANS:] = tail
    low_den[...] = jnp.ones_like(low_den)
    high_den[...] = jnp.ones_like(high_den)

    def prologue(r, side, start, size):
        vblk, qm, kts, gate = side
        at = slice(start, start + size)
        y = spread_norm(load_x(r, start, size), ones, gain_ref[...], shift_ref[...])
        proj = dot_nn(y, w_ref[...])
        q = proj[:, :CHANS] * (HEAD_DIM**-0.5 * LOG2E)
        v = proj[:, CHANS : 2 * CHANS]
        gate[at] = jax.nn.sigmoid(proj[:, 2 * CHANS :])
        kts[:, at] = dot_nt(wkt_ref[...], y).astype(BF)
        for h in range(HEADS):
            qm[h, at] = jnp.where(head_of == h, q, 0.0).astype(BF)
            vblk[h, at, :CHANS] = jnp.where(head_of == h, v, 0.0).astype(BF)

    def one_head(side, h, width):
        vblk, qm, kts, _ = side
        parts, size = [], width if flipped else width // 2
        for start in range(0, width, size):
            at = slice(start, start + size)
            s = dot_nn(qm[h, at], kts[:, :width]) + biasf[h, at, :width]
            parts.append(dot_nn(jnp.exp2(s).astype(BF), vblk[h, :width]))
        return jnp.concatenate(parts, 0)

    def finish_heads(acc, side, gated, width):
        den = acc[:, CHANS:]
        live = lax.broadcasted_iota(jnp.int32, (width, 1), 0) < n
        shown = jnp.where(live, den, 1.0).reshape(width // 8, 8, CHANS)
        low_den[...] = jnp.minimum(low_den[...], jnp.min(shown, 0))
        high_den[...] = jnp.maximum(high_den[...], jnp.max(shown, 0))
        gated[:width] = (acc[:, :CHANS] / den * side[3][:width]).astype(BF)

    def epilogue(r, gated, start, size):
        live = start + lax.broadcasted_iota(jnp.int32, (size, 1), 0) < n
        update = jnp.where(live, dot_nn(gated[start : start + size], wo_ref[...]), 0.0)
        result = (load_x(r, start, size).astype(F32) + update).astype(BF)
        normed = spread_norm(result, ones, gain2_ref[...], shift2_ref[...])
        wide = result.astype(F32)
        if flipped:
            hidden = jax.nn.relu(dot_nn(normed, extra_ref[...])).astype(BF)
            update = jnp.where(live, dot_nn(hidden, down_ref[...]), 0.0)
            put(r, start, wide + update)
        else:
            put(r, start, wide)
            mine = lax.broadcasted_iota(jnp.int32, (1, CHANS), 1) % ROWS == r
            spot = jnp.where(mine, extra_ref[...].astype(F32), 0.0).astype(BF)
            bias_rows[start : start + size] = jnp.where(
                mine, dot_nn(normed, spot), bias_rows[start : start + size]
            )

    def work(width):
        part = width // PARTS
        chunks = [c * part for c in range(PARTS)]

        def row(r, side, gated):
            for c in chunks:
                prologue(r, side, c, part)
            acc = one_head(side, 0, width)
            for h in range(1, HEADS):
                acc = acc + one_head(side, h, width)
            finish_heads(acc, side, gated, width)
            for c in chunks:
                epilogue(r, gated, c, part)

        def pro(r, side):
            for c in chunks:
                prologue(r, side, c, part)

        def att(side, gated, hook=None):
            acc = one_head(side, 0, width)
            for h in range(1, HEADS):
                if hook is not None:
                    hook(h)
                acc = acc + one_head(side, h, width)
            finish_heads(acc, side, gated, width)

        def epi(r, gated):
            for c in chunks:
                epilogue(r, gated, c, part)

        def pair(u, _):
            ra, rb = 2 * u, 2 * u + 1
            pro(ra, side_a)
            pro(rb, side_b)
            att(side_a, gated_a)
            att(side_b, gated_b)
            epi(ra, gated_a)
            epi(rb, gated_b)
            return 0

        lax.fori_loop(0, live_rows // 2, pair, 0)

        @pl.when(live_rows % 2 == 1)
        def _():
            row(live_rows - 1, side_a, gated_a)

        if width < RES:

            def rest(r, _):
                put(r, width, load_x(r, width, RES - width).astype(F32))
                return 0

            lax.fori_loop(0, live_rows, rest, 0)

        @pl.when(jnp.logical_not((jnp.min(low_den[...]) > DEN_LOW) & (jnp.max(high_den[...]) < DEN_HIGH)))
        def _():
            def careful(r, _):
                for c in chunks:
                    prologue(r, side_a, c, part)

                def block(t, _):
                    at = pl.ds(pl.multiple_of(t * 128, 128), 128)
                    acc = jnp.zeros((128, 2 * CHANS), F32)
                    for h in range(HEADS):
                        s = dot_nn(qm_a[h, at], kts_a[:, :width]) + biasf[h, at, :width]
                        s = s - jnp.max(s, -1, keepdims=True)
                        acc += dot_nn(jnp.exp2(s).astype(BF), vblk_a[h, :width])
                    gated_a[at] = (acc[:, :CHANS] / acc[:, CHANS:] * gate_a[at]).astype(BF)
                    return 0

                lax.fori_loop(0, width // 128, block, 0)
                for c in chunks:
                    epilogue(r, gated_a, c, part)
                return 0

            lax.fori_loop(0, live_rows, careful, 0)

    low = 0
    for width in WIDTHS:

        @pl.when((live_rows > 0) & (n > low) & (n <= width))
        def _(width=width):
            work(width)

        low = width

    def passed(r, _):
        put(r, 0, load_x(r, 0, RES).astype(F32))
        return 0

    lax.fori_loop(live_rows, count, passed, 0)

    def deliver(c, _):
        if flipped:
            size = ROWS * count * 2
            at = pl.ds(pl.multiple_of(c * size, size), size)
            out_ref[pl.ds(2 * c, 2)] = line[at].reshape(2, ROWS, count, CHANS).astype(BF)
        else:
            at = pl.ds(pl.multiple_of(c * RES, RES), RES)
            out_ref[:, c] = line[at].reshape(DEVS, ROWS, CHANS).astype(BF)
        return 0

    lax.fori_loop(0, ROWS, deliver, 0)
    if not flipped:
        for q in range(4):
            turned = bias_rows[q * CHANS : (q + 1) * CHANS].T
            for h in range(HEADS):
                piece = turned[h * ROWS : (h + 1) * ROWS].astype(BF)
                for e in range(h // 2, DEVS, 2):
                    out_ref[e, ROWS + (h % 2) * 4 + q] = piece


def attend(flipped, place, info, state, biases, gain, shift, gain2, shift2, w, wkt, wo, extra, down):
    whole = lambda a: pl.BlockSpec(a.shape, lambda i, s: (0,) * a.ndim)
    if flipped:
        column, count = place
        x_spec = pl.BlockSpec((DEVS, ROWS, ROWS, CHANS), lambda i, s: (0, 0, 0, 0))
        bias_specs = [
            pl.BlockSpec((DEVS, EXTRA, ROWS, CHANS), lambda i, s, at=at: (0, at, 0, 0))
            for _, at in biases
        ]
        out_shape = jax.ShapeDtypeStruct((DEVS, ROWS, count, CHANS), BF)
    else:
        column, count = 0, ROWS
        x_spec = pl.BlockSpec((None, ROWS, RES, CHANS), lambda i, s: (s[4], 0, 0, 0))
        bias_specs = [
            pl.BlockSpec((DEVS // 2, HEADS * ROWS, RES), lambda i, s, at=at: (at, 0, 0))
            for _, at in biases
        ]
        out_shape = jax.ShapeDtypeStruct((DEVS, ROWS + EXTRA, ROWS, CHANS), BF)
    twice = lambda shape, dtype: [pltpu.VMEM(shape, dtype)] * 2
    return pl.pallas_call(
        partial(attend_kernel, flipped, column, count),
        grid_spec=pltpu.PrefetchScalarGridSpec(
            num_scalar_prefetch=1,
            grid=(1,),
            in_specs=[x_spec]
            + bias_specs
            + [whole(a) for a in (gain, shift, gain2, shift2, w, wkt, wo, extra, down)],
            out_specs=whole(out_shape),
            scratch_shapes=[pltpu.VMEM((HEADS, RES, RES), F32)]
            + twice((HEADS, RES, 2 * CHANS), BF)
            + twice((HEADS, RES, CHANS), BF)
            + twice((CHANS, RES), BF)
            + twice((RES, CHANS), F32)
            + twice((RES, CHANS), BF)
            + [
                pltpu.VMEM((RES * count, CHANS), F32),
                pltpu.VMEM((RES, CHANS), F32),
            ]
            + twice((8, CHANS), F32),
        ),
        out_shape=out_shape,
        compiler_params=pltpu.CompilerParams(vmem_limit_bytes=VMEM_LIMIT),
        cost_estimate=pl.CostEstimate(
            flops=30_000_000_000, bytes_accessed=8_000_000, transcendentals=0
        ),
        name="attend_columns" if flipped else "attend_rows",
    )(info, state, biases[0][0], biases[1][0], gain, shift, gain2, shift2, w, wkt, wo, extra, down)


def tail_kernel(x_ref, *refs):
    refs[-1][...] = x_ref[...]


def bias_tail(state, after):
    shape = (DEVS, EXTRA, ROWS, CHANS)
    block = (DEVS // 4, EXTRA, ROWS, CHANS)
    return pl.pallas_call(
        tail_kernel,
        grid=(4,),
        in_specs=[pl.BlockSpec(block, lambda i: (i, ROWS // EXTRA, 0, 0))]
        + [pl.BlockSpec(memory_space=pl.ANY)] * len(after),
        out_specs=pl.BlockSpec(block, lambda i: (i, 0, 0, 0)),
        out_shape=jax.ShapeDtypeStruct(shape, BF),
        name="bias_tail",
    )(state, *after)


def join_kernel(_, x_ref, *refs):
    out_ref, line = refs[-2:]

    for i in range(out_ref.shape[0]):
        for e in range(DEVS):
            line[i, pl.ds(e, ROWS, stride=DEVS), :] = x_ref[e, i].astype(F32)
    for i in range(out_ref.shape[0]):
        out_ref[i] = line[i].astype(BF)


def join(info, state, earlier):
    more = [] if earlier is None else [earlier]
    part = ROWS // 4
    return pl.pallas_call(
        join_kernel,
        grid_spec=pltpu.PrefetchScalarGridSpec(
            num_scalar_prefetch=1,
            grid=(ROWS // part,),
            in_specs=[pl.BlockSpec((DEVS, part, ROWS, CHANS), lambda i, s: (0, i, 0, 0))]
            + [pl.BlockSpec(memory_space=pl.ANY)] * len(more),
            out_specs=pl.BlockSpec((None, part, RES, CHANS), lambda i, s: (s[4], i, 0, 0)),
            scratch_shapes=[pltpu.VMEM((part, RES, CHANS), F32)],
        ),
        out_shape=jax.ShapeDtypeStruct((2, ROWS, RES, CHANS), BF),
        input_output_aliases={2: 0} if more else {},
        compiler_params=pltpu.CompilerParams(vmem_limit_bytes=VMEM_LIMIT),
        name="join",
    )(info, state, *more)


def shifted(state, dy, dz, dc):
    return lax.ppermute(
        state,
        "dap",
        [
            ((y * 4 + z) * 2 + c, ((y + dy) % 4 * 4 + (z + dz) % 4) * 2 + (c ^ dc))
            for y in range(4)
            for z in range(4)
            for c in range(2)
        ],
    )


SHIFTS = (0, 1, -1, 2)


def stack_kernel(*refs):
    out_ref = refs[-1]
    for t in range(len(SHIFTS)):
        out_ref[t] = refs[t][...]


def stack_blocks(blocks, after):
    return pl.pallas_call(
        stack_kernel,
        in_specs=[pl.BlockSpec(memory_space=pltpu.VMEM)] * len(blocks)
        + [pl.BlockSpec(memory_space=pl.ANY)],
        out_specs=pl.BlockSpec(memory_space=pltpu.VMEM),
        out_shape=jax.ShapeDtypeStruct((len(blocks),) + blocks[0].shape, BF),
        name="stack_blocks",
    )(*blocks, after)


def gather_steps(local, after):
    line = stack_blocks([local] + [shifted(local, 0, k, 0) for k in SHIFTS[1:]], after)
    plane = jnp.concatenate([line] + [shifted(line, k, 0, 0) for k in SHIFTS[1:]])
    return plane, shifted(plane, 0, 0, 1)


def gather_order(me):
    y, z, c = me // 8, me // 2 % 4, me % 2
    order = [
        ((y - ky) % 4 * 4 + (z - kz) % 4) * 2 + (c ^ other if other else c)
        for other in range(2)
        for ky in SHIFTS
        for kz in SHIFTS
    ]
    return [jnp.asarray(v, jnp.int32) for v in order]


def swap_blocks(state):
    return lax.all_to_all(state, "dap", 0, 0, tiled=True)


def on_device(
    pair_state, lengths, norm_gain, norm_shift, attn_proj, bias_proj, attn_out, trans_up, trans_down
):
    group = lax.axis_index("grp")
    me = lax.axis_index("dap")
    pairs = pair_state.shape[0]
    gains = [norm_gain[m : m + 1] for m in range(3)]
    shifts = [norm_shift[m : m + 1] for m in range(3)]
    w_qvg = [
        jnp.concatenate([attn_proj[m, :, :CHANS], attn_proj[m, :, 2 * CHANS :]], 1)
        for m in range(2)
    ]
    w_kt = [attn_proj[m, :, CHANS : 2 * CHANS].T for m in range(2)]
    bpt = [jnp.pad(bias_proj[m].T, ((0, 16 - HEADS), (0, 0))) for m in range(2)]
    own = [lax.dynamic_index_in_dim(lengths, group * pairs + p, 0, keepdims=False) for p in range(pairs)]
    turned = (own[1] > own[0]).astype(jnp.int32)
    lens = [jnp.maximum(own[0], own[1]), jnp.minimum(own[0], own[1])]
    members = [turned, 1 - turned]
    bias_spread = jnp.pad(jnp.repeat(bias_proj[1], ROWS, 1), ((0, 0), (0, CHANS - HEADS * ROWS)))
    parity = me % 2
    order = [gather_order(me)] + [list(range(DEVS))] * (pairs - 1)
    row_info = [
        jnp.stack([jnp.asarray(v, jnp.int32) for v in [n, me * ROWS, 1, parity, at] + o])
        for n, at, o in zip(lens, members, order)
    ]
    col_info = [
        jnp.stack([jnp.asarray(v, jnp.int32) for v in [n, me, DEVS, parity, at]])
        for n, at in zip(lens, members)
    ]

    bias0 = [first_bias(members[p][None], pair_state, gains[0], shifts[0], bpt[0]) for p in range(pairs)]
    first_plane, second_plane = gather_steps(bias0[0], bias0[1])
    whole_bias = lax.all_gather(bias0[1], "dap", axis=0)
    biases = [[(first_plane, 0), (second_plane, 0)], [(whole_bias, 0), (whole_bias, 1)]]
    firsts, moved = [], []
    for p in range(pairs):
        first = attend(
            False, None, row_info[p], pair_state, biases[p], gains[0], shifts[0], gains[1], shifts[1],
            w_qvg[0], w_kt[0], attn_out[0], bias_spread, trans_down,
        )
        firsts.append(first)
        moved.append(swap_blocks(first))
    result, third = None, firsts[-1]
    for p in range(pairs):
        other = shifted(bias_tail(moved[p], [third]), 0, 0, 1)
        third = attend(
            True, (0, ROWS), col_info[p], moved[p], [(moved[p], 2), (other, 0)], gains[1], shifts[1],
            gains[2], shifts[2], w_qvg[1], w_kt[1], attn_out[1], trans_up, trans_down,
        )
        result = join(col_info[p], swap_blocks(third), result)
    return result


def solution(mesh):
    in_specs = (P("grp", "dap", None, None), P(), P(), P(), P(), P(), P(), P(), P())
    out_specs = P("grp", "dap", None, None)
    return jax.shard_map(
        on_device, mesh=mesh, in_specs=in_specs, out_specs=out_specs, check_vma=False
    )
```
